512 devices in a mesh: ctx: 64 (over z, y), kvh: 8 (over x, core).
Axes of the slice: x: 4, y: 8, z: 8, core: 2. Of those that a mesh axis runs over, the one named last changes fastest.
Arguments:
- queries: bfloat16 [1024, 128, 128], P(('ctx', 'kvh')), may hold values from -6 to 6
- new_keys: bfloat16 [1024, 8, 128], P('ctx', 'kvh'), may hold values from -6 to 6
- new_values: bfloat16 [1024, 8, 128], P('ctx', 'kvh'), may hold values from -6 to 6
- new_positions: int32 [1024], P('ctx'), may hold values from 0 to 1023, each once
- hist_keys: bfloat16 [192, 128, 8, 128], P('ctx', None, 'kvh'), may hold values from -6 to 6
- hist_values: bfloat16 [192, 128, 8, 128], P('ctx', None, 'kvh'), may hold values from -6 to 6
- page_slots: int32 [128], replicated, may hold values from 0 to 191, as said below
Outputs:
- attention: bfloat16 [1024, 128, 128], P(('ctx', 'kvh'))
The draws below stay inside these ranges and needn't reach their ends.
Inputs may be any that keep to these rules, and one draw needn't show every extreme that they name: `page_slots`: entry p equals 3 * d + s: history page p is held in slot s of index d of ctx. Page p belongs to index p // 2, and d is that index or the one 64 // 2 away; an index holds at most one page that belongs to that other index and at most 3 pages in all; no slot holds two pages; slots that hold no page carry data that is not part of the history.
All inputs are finite; a program needn't handle non-finite values.
Results may differ from the reference program's by a relative error of at most 0.01.
Values may be sent and summed in bfloat16 or wider, within the bound.
No kernel may reach another device: no remote copies, remote signals or barrier semaphores. Data moves between devices by JAX's collectives and lax.ppermute only.
A program may use at most 64 MiB of HBM per device.

```python
import math
import jax
import jax.numpy as jnp
from jax import lax

QH = 128
KVH = 8
HD = 128
PAGE = 128
PAGES_DEV = 2
SLOTS_DEV = 3
NEW = 1024
PAGES = 128
N_CTX = 64


def draw_queries(key, part):
    key = jax.random.fold_in(key, 1)
    sample = jnp.clip(jax.random.normal(key, (NEW, QH, HD), jnp.float32), -6.0, 6.0)
    return sample.astype(jnp.bfloat16)


def draw_hist_keys(key, part):
    key = jax.random.fold_in(key, 2)
    sample = jnp.clip(jax.random.normal(key, (N_CTX * SLOTS_DEV, PAGE, KVH, HD), jnp.float32), -6.0, 6.0)
    return sample.astype(jnp.bfloat16)


def draw_page_slots(key, part):
    key = jax.random.fold_in(key, 3)
    subkeys = jax.random.split(key, 2)
    half_cycle = N_CTX // 2
    pair_index = jnp.arange(half_cycle)
    upper_hot = jax.random.randint(subkeys[0], (half_cycle,), 0, 2)
    upper_hot = upper_hot.at[0].set(0).at[half_cycle - 1].set(1)
    hot_dev = pair_index + half_cycle * upper_hot
    cold_dev = pair_index + half_cycle * (1 - upper_hot)
    rotation = jax.random.randint(subkeys[1], (N_CTX,), 0, SLOTS_DEV)
    page_index = jnp.arange(PAGES_DEV)

    def slot_of(device, base):
        return device * SLOTS_DEV + (base + rotation[device]) % SLOTS_DEV
    hot_pages = hot_dev[:, None] * PAGES_DEV + page_index[None, :]
    hot_slots = slot_of(hot_dev[:, None], page_index[None, :])
    cold_pages = cold_dev[:, None] * PAGES_DEV + page_index[None, :]
    moved_slot = slot_of(hot_dev[:, None], PAGES_DEV + 0 * page_index[None, :])
    kept_slot = slot_of(cold_dev[:, None], page_index[None, :])
    cold_slots = jnp.where(page_index[None, :] == PAGES_DEV - 1, moved_slot, kept_slot)
    result = jnp.zeros((PAGES,), jnp.int32)
    result = result.at[hot_pages.reshape(-1)].set(hot_slots.reshape(-1).astype(jnp.int32))
    result = result.at[cold_pages.reshape(-1)].set(cold_slots.reshape(-1).astype(jnp.int32))
    return result


def block_scale(own_key, extent, cuts, smallest, high):
    def one(dim, parts):
        heights = jax.random.uniform(jax.random.fold_in(jax.random.fold_in(own_key, 6), dim), (parts,), jnp.float32, smallest / len(cuts), high / len(cuts))
        return jnp.repeat(jnp.exp(heights), extent[dim] // parts).reshape((-1,) + (1,) * (len(extent) - dim - 1))

    loudness = one(*cuts[0])
    for cut in cuts[1:]:
        loudness = loudness * one(*cut)
    return loudness


def gaussian(key, shape, scale, reach, shards=(), kind=jnp.bfloat16):
    values = jax.random.normal(key, shape, jnp.float32) * scale
    if len(shards) > 0:
        values = block_scale(key, shape, shards, -0.22, 0.18) * values
    return jnp.clip(values, min=-reach, max=reach).astype(kind)


def setup_inputs(seed: int = 0) -> dict:
    streams_of = jax.random.split(jax.random.key(seed), 8)
    return {
        "queries": draw_queries(jax.random.fold_in(streams_of[7], 71), 0),
        "new_keys": gaussian(streams_of[1], (NEW, KVH, HD), 1.0, 6.0, ((0, 64), (1, 8))),
        "new_values": gaussian(streams_of[2], (NEW, KVH, HD), 1.0, 6.0, ((0, 64), (1, 8))),
        "new_positions": jax.random.permutation(streams_of[3], NEW).astype(jnp.int32),
        "hist_keys": draw_hist_keys(jax.random.fold_in(streams_of[7], 71), 0),
        "hist_values": gaussian(streams_of[5], (N_CTX * SLOTS_DEV, PAGE, KVH, HD), 1.0, 6.0, ((0, 64), (2, 8))),
        "page_slots": draw_page_slots(jax.random.fold_in(streams_of[7], 71), 0),
    }


def attend_rows(query_rows, key_rows, value_rows, visible):
    tokens_here, per_group, width = query_rows.shape
    flat = query_rows.reshape(tokens_here * per_group, width)
    scores = jnp.dot(flat, key_rows.T, preferred_element_type=jnp.float32)
    scores = scores.reshape(tokens_here, per_group, -1) * (1.0 / math.sqrt(width))
    masked_in = visible[:, None, :]
    scores = jnp.where(masked_in, scores, -1e+30)
    row_max = lax.optimization_barrier(jnp.max(scores, axis=-1, keepdims=True))
    weights = jnp.where(masked_in, jnp.exp(scores - row_max), 0.0)
    totals = lax.optimization_barrier(jnp.sum(weights, axis=-1))
    rounded = weights.astype(jnp.bfloat16).reshape(tokens_here * per_group, -1)
    summed = jnp.dot(rounded, value_rows, preferred_element_type=jnp.float32)
    summed = summed.reshape(tokens_here, per_group, width) / totals[..., None]
    return summed.astype(jnp.bfloat16)

def reference(queries, new_keys, new_values, new_positions, hist_keys, hist_values, page_slots):
    history_keys = hist_keys[page_slots].reshape(-1, KVH, HD)
    history_values = hist_values[page_slots].reshape(-1, KVH, HD)
    all_keys = jnp.concatenate([history_keys, new_keys], axis=0)
    all_values = jnp.concatenate([history_values, new_values], axis=0)
    hist_len = history_keys.shape[0]
    group_size = QH // KVH
    block_len = math.gcd(NEW, 128)
    block_count = NEW // block_len
    grouped = queries.reshape(NEW, KVH, group_size, HD).transpose(1, 0, 2, 3)
    keys_by_head = all_keys.transpose(1, 0, 2)
    values_by_head = all_values.transpose(1, 0, 2)
    position_blocks = new_positions.reshape(block_count, block_len)
    history_seen = jnp.ones((block_len, hist_len), dtype=bool)

    def per_head(operands):
        head_queries, head_keys, head_values = operands

        def per_block(pieces):
            query_block, position_block = pieces
            fresh_seen = new_positions[None, :] <= position_block[:, None]
            visible = jnp.concatenate([history_seen, fresh_seen], axis=1)
            return attend_rows(query_block, head_keys, head_values, visible)
        blocks = head_queries.reshape(block_count, block_len, group_size, HD)
        result = lax.map(per_block, (blocks, position_blocks))
        return result.reshape(NEW, group_size, HD)
    outputs = lax.map(per_head, (grouped, keys_by_head, values_by_head))
    return outputs.transpose(1, 0, 2, 3).reshape(NEW, QH, HD)
```

```python
import functools
import math

import jax
import jax.numpy as jnp
from jax import lax
from jax.experimental import pallas as pl
from jax.experimental.pallas import tpu as pltpu
from jax.sharding import Mesh, PartitionSpec as P

ZN, YN, XN, CN = 8, 8, 4, 2
KN = XN * CN
HEADS, GROUP, HD, PAGE, SLOTS, NEWT = 128, 16, 128, 128, 3, 16
HISTORY = SLOTS * PAGE
KV_ROWS = HISTORY + 2 * NEWT
PAGES = 2 * ZN
KEYS = PAGES * PAGE + ZN * NEWT
OWN = 2
BLOCK = OWN * GROUP
WIRE = BLOCK + 8
ALL_BLOCKS = YN * KN
STEP_BLOCKS = 16
ROWS = STEP_BLOCKS * BLOCK
CHUNKS = ((0, 512), (512, 512), (1024, 512), (1536, 512), (2048, 128))
TO_BITS = math.log2(math.e) / math.sqrt(HD)
LOWEST = -1e30


def attend_kernel(slots, kv, q, out, keys, values, key_positions, scores):
    @pl.when(pl.program_id(0) == 0)
    def _():
        for i in range(PAGES):
            slot = slots[i]
            source = slot // SLOTS
            first = pl.multiple_of((slot % SLOTS) * PAGE, PAGE)
            keys[i * PAGE : (i + 1) * PAGE, :] = kv[source, 0, pl.ds(first, PAGE), :]
            values[i * PAGE : (i + 1) * PAGE, :HD] = kv[source, 1, pl.ds(first, PAGE), :]
        base = PAGES * PAGE
        for z in range(ZN):
            here = slice(base + z * NEWT, base + (z + 1) * NEWT)
            keys[here, :] = kv[z, 0, HISTORY : HISTORY + NEWT, :]
            values[here, :HD] = kv[z, 1, HISTORY : HISTORY + NEWT, :]
        values[:, HD:] = jnp.ones((KEYS, HD), jnp.bfloat16)
        high = kv[:, 0, HISTORY + NEWT :, :].astype(jnp.float32)
        low = kv[:, 1, HISTORY + NEWT :, :].astype(jnp.float32)
        key_positions[...] = jnp.sum(high * 32.0 + low, axis=0)[:8]

    rows = q[:, :BLOCK, :].reshape(ROWS, HD)
    tags = q[:, BLOCK:, :].astype(jnp.float32)
    key_at = key_positions[0:1, :]
    bias = []
    for t in range(OWN):
        query_at = tags[:, 2 * t, :] * 32.0 + tags[:, 2 * t + 1, :]
        hidden = jnp.where(key_at <= query_at, 0.0, LOWEST)
        bias.append(jnp.broadcast_to(hidden[:, None, :], (STEP_BLOCKS, GROUP, HD)))
    bias = jnp.stack(bias, axis=1).reshape(ROWS, HD)
    top = None
    for start, size in CHUNKS:
        part = lax.dot_general(
            rows, keys[start : start + size, :], (((1,), (1,)), ((), ())), preferred_element_type=jnp.float32
        )
        if size == ZN * NEWT:
            part = part + bias
        scores[:, start : start + size] = part
        for j in range(size // HD):
            piece = part[:, j * HD : (j + 1) * HD]
            top = piece if top is None else jnp.maximum(top, piece)
    top = jnp.max(top, axis=1, keepdims=True) * TO_BITS
    summed = jnp.zeros((ROWS, 2 * HD), jnp.float32)
    for start, size in CHUNKS:
        weights = jnp.exp2(scores[:, start : start + size] * TO_BITS - top).astype(jnp.bfloat16)
        summed += jnp.dot(weights, values[start : start + size, :], preferred_element_type=jnp.float32)
    total = summed[:, HD:]
    out[:, :BLOCK, :] = (summed[:, :HD] / total).astype(jnp.bfloat16).reshape(STEP_BLOCKS, BLOCK, HD)
    level = (top + jnp.log2(total)).reshape(STEP_BLOCKS, BLOCK, HD)
    row = lax.broadcasted_iota(jnp.int32, (STEP_BLOCKS, BLOCK, HD), 1)
    lane = lax.broadcasted_iota(jnp.int32, (STEP_BLOCKS, BLOCK, HD), 2)
    level = jnp.sum(jnp.where(row == lane, level, 0.0), axis=1, keepdims=True)
    high = level.astype(jnp.bfloat16).astype(jnp.float32)
    rest = level - high
    middle = rest.astype(jnp.bfloat16).astype(jnp.float32)
    zeros = jnp.zeros((STEP_BLOCKS, 5, HD), jnp.float32)
    out[:, BLOCK:, :] = jnp.concatenate([high, middle, rest - middle, zeros], axis=1).astype(jnp.bfloat16)


def attend(slots, kv, q):
    return pl.pallas_call(
        attend_kernel,
        out_shape=jax.ShapeDtypeStruct((ALL_BLOCKS, WIRE, HD), jnp.bfloat16),
        grid_spec=pltpu.PrefetchScalarGridSpec(
            num_scalar_prefetch=1,
            grid=(ALL_BLOCKS // STEP_BLOCKS,),
            in_specs=[
                pl.BlockSpec((ZN, 2, KV_ROWS, HD), lambda i, s: (0, 0, 0, 0)),
                pl.BlockSpec((STEP_BLOCKS, WIRE, HD), lambda i, s: (i, 0, 0)),
            ],
            out_specs=pl.BlockSpec((STEP_BLOCKS, WIRE, HD), lambda i, s: (i, 0, 0)),
            scratch_shapes=[
                pltpu.VMEM((KEYS, HD), jnp.bfloat16),
                pltpu.VMEM((KEYS, 2 * HD), jnp.bfloat16),
                pltpu.VMEM((8, HD), jnp.float32),
                pltpu.VMEM((ROWS, KEYS), jnp.float32),
            ],
        ),
        compiler_params=pltpu.CompilerParams(vmem_limit_bytes=40 * 1024 * 1024),
        cost_estimate=pl.CostEstimate(flops=2300000000, bytes_accessed=4000000, transcendentals=4456448),
    )(slots, kv, q)


def combine_kernel(parts, out):
    tags = parts[:, BLOCK:, :].astype(jnp.float32)
    level = tags[:, 0:1, :] + tags[:, 1:2, :] + tags[:, 2:3, :]
    level = level.reshape(YN, KN, 1, HD)
    weight = jnp.exp2(level - jnp.max(level, axis=0, keepdims=True))
    weight = weight / jnp.sum(weight, axis=0, keepdims=True)
    row = lax.broadcasted_iota(jnp.int32, (BLOCK, HD), 0)
    lane = lax.broadcasted_iota(jnp.int32, (BLOCK, HD), 1)
    for k in range(KN):
        merged = jnp.zeros((BLOCK, HD), jnp.float32)
        for y in range(YN):
            column = jnp.sum(jnp.where(row == lane, weight[y, k], 0.0), axis=1, keepdims=True)
            merged += column * parts[y * KN + k, :BLOCK, :].astype(jnp.float32)
        merged = merged.astype(jnp.bfloat16)
        for t in range(OWN):
            out[t, k * GROUP : (k + 1) * GROUP, :] = merged[t * GROUP : (t + 1) * GROUP, :]


def combine(parts):
    return pl.pallas_call(
        combine_kernel,
        out_shape=jax.ShapeDtypeStruct((OWN, HEADS, HD), jnp.bfloat16),
        compiler_params=pltpu.CompilerParams(vmem_limit_bytes=16 * 1024 * 1024),
        cost_estimate=pl.CostEstimate(flops=1000000, bytes_accessed=800000, transcendentals=8192),
    )(parts)


def body(queries, new_keys, new_values, new_positions, hist_keys, hist_values, page_slots):
    z, y = lax.axis_index("z"), lax.axis_index("y")
    k = lax.axis_index(("x", "c"))
    high = (new_positions // 32).astype(jnp.bfloat16)
    low = (new_positions % 32).astype(jnp.bfloat16)

    def with_tag(history, fresh, tag):
        placed = lax.dynamic_update_slice(jnp.zeros((1, HD), jnp.bfloat16), tag[None, :], (0, z * NEWT))
        return jnp.concatenate(
            [history.reshape(HISTORY, HD), fresh.reshape(NEWT, HD), placed, jnp.zeros((NEWT - 1, HD), jnp.bfloat16)]
        )

    kv = jnp.stack([with_tag(hist_keys, new_keys, high), with_tag(hist_values, new_values, low)])
    kv = lax.all_gather(kv, "z", axis=0, tiled=False)
    held = lax.dynamic_index_in_dim(page_slots.reshape(ZN, YN, 2), y, 1, keepdims=False).reshape(PAGES)
    slots = (held // (SLOTS * YN)) * SLOTS + held % SLOTS

    own_high = lax.dynamic_slice_in_dim(high, k * OWN, OWN)
    own_low = lax.dynamic_slice_in_dim(low, k * OWN, OWN)
    tag = jnp.stack([own_high[0], own_low[0], own_high[1], own_low[1]] + [jnp.zeros((), jnp.bfloat16)] * 4)
    sent = queries.reshape(OWN, KN, GROUP, HD).transpose(1, 0, 2, 3).reshape(KN, BLOCK, HD)
    sent = jnp.concatenate([sent, jnp.broadcast_to(tag[None, :, None], (KN, 8, HD))], axis=1)
    sent = jnp.broadcast_to(sent[None], (YN, KN, WIRE, HD)).reshape(ALL_BLOCKS, WIRE, HD)
    q = lax.all_to_all(sent, ("y", "x", "c"), split_axis=0, concat_axis=0, tiled=True)
    parts = attend(slots, kv, q)
    parts = lax.all_to_all(parts, ("y", "x", "c"), split_axis=0, concat_axis=0, tiled=True)
    return combine(parts)


def solution(mesh):
    split = Mesh(mesh.devices.reshape(ZN, YN, XN, CN), ("z", "y", "x", "c"))
    ctx, kvh = ("z", "y"), ("x", "c")
    in_specs = (
        P(ctx + kvh, None, None),
        P(ctx, kvh, None),
        P(ctx, kvh, None),
        P(ctx),
        P(ctx, None, kvh, None),
        P(ctx, None, kvh, None),
        P(),
    )
    return jax.shard_map(body, mesh=split, in_specs=in_specs, out_specs=P(ctx + kvh, None, None), check_vma=False)
```

```python
import functools
import math

import jax
import jax.numpy as jnp
import numpy as np
from jax import lax
from jax.experimental import pallas as pl
from jax.experimental.pallas import tpu as pltpu
from jax.sharding import Mesh, PartitionSpec as P

ZN, YN, XN, CN = 8, 8, 4, 2
LINE = 8
ALL = ("z", "y", "x", "c")
HEADS, GROUP, HD, PAGE, SLOTS, NEWT = 128, 16, 128, 128, 3, 16
HISTORY = SLOTS * PAGE
KV_ROWS = HISTORY + 2 * NEWT
FRESH = LINE * NEWT
MOST_PAGES = LINE * SLOTS
KEYS = FRESH + MOST_PAGES * PAGE
OWN = 2
TOKENS = OWN * CN
BLOCK = TOKENS * GROUP
WIRE = BLOCK + 8
BLOCKS = LINE * XN
STEP_BLOCKS = 8
ROWS = STEP_BLOCKS * BLOCK
OFFSETS = (0, -3, 3, -1, -4, 2, 1, -2)
TO_BITS = math.log2(math.e) / math.sqrt(HD)
LOWEST = -1e30

IDS = np.arange(ZN * YN * XN * CN).reshape(ZN, YN, XN, CN)
CROSS = [IDS[z, :, :, 0].ravel().tolist() for z in range(ZN)] + [IDS[:, y, :, 1].ravel().tolist() for y in range(YN)]


def along(distance):
    route = []
    for z in range(ZN):
        for y in range(YN):
            for x in range(XN):
                route.append((int(IDS[z, y, x, 0]), int(IDS[(z + distance) % ZN, y, x, 0])))
                route.append((int(IDS[z, y, x, 1]), int(IDS[z, (y + distance) % YN, x, 1])))
    return route


SWAP = [(int(i), int(i) ^ 1) for i in IDS.ravel()]


def call(kernel, out_shape, megabytes=16, flops=1000000, moved=800000, **options):
    return pl.pallas_call(
        kernel,
        out_shape=out_shape,
        compiler_params=pltpu.CompilerParams(vmem_limit_bytes=megabytes * 1024 * 1024),
        cost_estimate=pl.CostEstimate(flops=flops, bytes_accessed=moved, transcendentals=flops // 500),
        **options,
    )


def bf16(*shape):
    return jax.ShapeDtypeStruct(shape, jnp.bfloat16)


SMEM = pl.BlockSpec(memory_space=pltpu.SMEM)
VMEM = pl.BlockSpec(memory_space=pltpu.VMEM)


def pack_kernel(place, positions, queries, hist_keys, hist_values, new_keys, new_values, kv, kept, sent):
    core, line = place[0], place[1]
    for side, (history, fresh) in enumerate(((hist_keys, new_keys), (hist_values, new_values))):
        kv[side, :HISTORY, :] = history[...]
        kv[side, HISTORY : HISTORY + NEWT, :] = fresh[...]
        lane = lax.broadcasted_iota(jnp.int32, (NEWT, HD), 1)
        tag = jnp.zeros((NEWT, HD), jnp.int32)
        for i in range(NEWT):
            digit = positions[i] // 32 if side == 0 else positions[i] % 32
            tag = jnp.where(lane == line * NEWT + i, digit, tag)
        kv[side, HISTORY + NEWT :, :] = tag.astype(jnp.float32).astype(jnp.bfloat16)
    for target, parity in ((kept, core), (sent, 1 - core)):
        for t in range(OWN):
            for x in range(XN):
                first = pl.multiple_of((CN * x + parity) * GROUP, GROUP)
                target[t, x] = queries[t, pl.ds(first, GROUP), :]


def spread_kernel(place, positions, kept, received, out):
    core, x_here = place[0], place[2]
    row = lax.broadcasted_iota(jnp.int32, (8, HD), 0)
    tag = jnp.zeros((8, HD), jnp.int32)
    for i in range(TOKENS):
        position = positions[x_here * TOKENS + i]
        tag = jnp.where(row == 2 * i, position // 32, tag)
        tag = jnp.where(row == 2 * i + 1, position % 32, tag)
    tag = tag.astype(jnp.float32).astype(jnp.bfloat16)
    for x in range(XN):
        for other, array in ((0, kept), (1, received)):
            owner = core if other == 0 else 1 - core
            rows = array[:, x].reshape(OWN * GROUP, HD)
            first = pl.multiple_of(owner * OWN * GROUP, OWN * GROUP)
            for line in range(LINE):
                out[line * XN + x, pl.ds(first, OWN * GROUP), :] = rows
        for line in range(LINE):
            out[line * XN + x, BLOCK:, :] = tag


def join_kernel(own, lower, upper, three, two):
    for i, block in enumerate((own, lower, upper)):
        three[i] = block[...]
        if i < 2:
            two[i] = block[...]


def attend_kernel(
    place, page_slots, own, lower, upper, below, above, q, out, keys, values, key_positions, scores, found
):
    core, line, ctx = place[0], place[1], place[3]

    @pl.when(pl.program_id(0) == 0)
    def _():
        values[:, HD:] = jnp.ones((KEYS, HD), jnp.bfloat16)
        blocks = [own, lower, upper] + [below.at[i] for i in range(3)] + [above.at[i] for i in range(2)]
        stride = jnp.where(core == 0, YN, 1)
        high = jnp.zeros((NEWT, HD), jnp.float32)
        low = jnp.zeros((NEWT, HD), jnp.float32)
        count = jnp.int32(0)
        for block, offset in zip(blocks, OFFSETS, strict=True):
            source_line = lax.rem(line + offset + LINE, LINE)
            source = ctx + (source_line - line) * stride
            other = lax.rem(source + ZN * YN // 2, ZN * YN)
            first = pl.multiple_of(source_line * NEWT, NEWT)
            keys[pl.ds(first, NEWT), :] = block[0, HISTORY : HISTORY + NEWT, :]
            values[pl.ds(first, NEWT), :HD] = block[1, HISTORY : HISTORY + NEWT, :]
            high += block[0, HISTORY + NEWT :, :].astype(jnp.float32)
            low += block[1, HISTORY + NEWT :, :].astype(jnp.float32)
            candidates = [page_slots[2 * source], page_slots[2 * source + 1]]
            candidates += [page_slots[2 * other], page_slots[2 * other + 1]]
            for s in range(SLOTS):
                slot = source * SLOTS + s
                live = functools.reduce(jnp.logical_or, [candidate == slot for candidate in candidates])
                to = pl.multiple_of(FRESH + count * PAGE, PAGE)

                @pl.when(live)
                def _(block=block, s=s, to=to):
                    keys[pl.ds(to, PAGE), :] = block[0, s * PAGE : (s + 1) * PAGE, :]
                    values[pl.ds(to, PAGE), :HD] = block[1, s * PAGE : (s + 1) * PAGE, :]

                count += live.astype(jnp.int32)
        key_positions[...] = (high * 32.0 + low)[:8]
        found[0] = count
        for i in range(1, MOST_PAGES):

            @pl.when(i >= count)
            def _(i=i):
                here = slice(FRESH + i * PAGE, FRESH + (i + 1) * PAGE)
                keys[here, :] = keys[FRESH : FRESH + PAGE, :]
                values[here, :] = jnp.zeros((PAGE, 2 * HD), jnp.bfloat16)

    count = found[0]

    def attend_to(pages):
        chunks = [(0, FRESH + 3 * PAGE)]
        while sum(chunks[-1]) < FRESH + pages * PAGE:
            start = sum(chunks[-1])
            chunks.append((start, min(4 * PAGE, FRESH + pages * PAGE - start)))
        rows = q[:, :BLOCK, :].reshape(ROWS, HD)
        tags = q[:, BLOCK:, :].astype(jnp.float32)
        key_at = key_positions[0:1, :]
        bias = []
        for t in range(TOKENS):
            query_at = tags[:, 2 * t, :] * 32.0 + tags[:, 2 * t + 1, :]
            hidden = jnp.where(key_at <= query_at, 0.0, LOWEST)
            bias.append(jnp.broadcast_to(hidden[:, None, :], (STEP_BLOCKS, GROUP, HD)))
        bias = jnp.stack(bias, axis=1).reshape(ROWS, HD)
        top = None
        for start, size in chunks:
            part = lax.dot_general(
                rows, keys[start : start + size, :], (((1,), (1,)), ((), ())), preferred_element_type=jnp.float32
            )
            for j in range(size // HD):
                piece = part[:, j * HD : (j + 1) * HD]
                if start + j == 0:
                    piece = piece + bias
                scores[:, start + j * HD : start + (j + 1) * HD] = piece
                top = piece if top is None else jnp.maximum(top, piece)
        top = jnp.max(top, axis=1, keepdims=True) * TO_BITS
        summed = jnp.zeros((ROWS, 2 * HD), jnp.float32)
        for start, size in chunks:
            weights = jnp.exp2(scores[:, start : start + size] * TO_BITS - top).astype(jnp.bfloat16)
            summed += jnp.dot(weights, values[start : start + size, :], preferred_element_type=jnp.float32)
        total = summed[:, HD:]
        out[:, :BLOCK, :] = (summed[:, :HD] / total).astype(jnp.bfloat16).reshape(STEP_BLOCKS, BLOCK, HD)
        level = (top + jnp.log2(total)).reshape(STEP_BLOCKS, BLOCK, HD)
        row = lax.broadcasted_iota(jnp.int32, (STEP_BLOCKS, BLOCK, HD), 1)
        lane = lax.broadcasted_iota(jnp.int32, (STEP_BLOCKS, BLOCK, HD), 2)
        level = jnp.sum(jnp.where(row == lane, level, 0.0), axis=1, keepdims=True)
        high = level.astype(jnp.bfloat16).astype(jnp.float32)
        rest = level - high
        middle = rest.astype(jnp.bfloat16).astype(jnp.float32)
        zeros = jnp.zeros((STEP_BLOCKS, 5, HD), jnp.float32)
        out[:, BLOCK:, :] = jnp.concatenate([high, middle, rest - middle, zeros], axis=1).astype(jnp.bfloat16)

    usual, larger = 2 * LINE, 2 * LINE + LINE // 2
    pl.when(count <= usual)(lambda: attend_to(usual))
    pl.when((count > usual) & (count <= larger))(lambda: attend_to(larger))
    pl.when(count > larger)(lambda: attend_to(MOST_PAGES))


def attend(place, page_slots, pieces, q):
    def whole(array):
        return pl.BlockSpec(array.shape, lambda i, *_: (0,) * array.ndim)

    wire = pl.BlockSpec((STEP_BLOCKS, WIRE, HD), lambda i, *_: (i, 0, 0))
    return call(
        attend_kernel,
        bf16(BLOCKS, WIRE, HD),
        megabytes=40,
        flops=2300000000,
        moved=5000000,
        grid_spec=pltpu.PrefetchScalarGridSpec(
            num_scalar_prefetch=2,
            grid=(BLOCKS // STEP_BLOCKS,),
            in_specs=[whole(piece) for piece in pieces] + [wire],
            out_specs=wire,
            scratch_shapes=[
                pltpu.VMEM((KEYS, HD), jnp.bfloat16),
                pltpu.VMEM((KEYS, 2 * HD), jnp.bfloat16),
                pltpu.VMEM((8, HD), jnp.float32),
                pltpu.VMEM((ROWS, KEYS), jnp.float32),
                pltpu.SMEM((1,), jnp.int32),
            ],
        ),
    )(place, page_slots, *pieces, q)


def combine_kernel(place, parts, kept, sent, merged_rows):
    core = place[0]
    tags = parts[:, BLOCK:, :].astype(jnp.float32)
    level = tags[:, 0:1, :] + tags[:, 1:2, :] + tags[:, 2:3, :]
    level = level.reshape(LINE, XN, 1, HD)
    weight = jnp.exp2(level - jnp.max(level, axis=0, keepdims=True))
    weight = weight / jnp.sum(weight, axis=0, keepdims=True)
    row = lax.broadcasted_iota(jnp.int32, (BLOCK, HD), 0)
    lane = lax.broadcasted_iota(jnp.int32, (BLOCK, HD), 1)
    for x in range(XN):
        merged = jnp.zeros((BLOCK, HD), jnp.float32)
        for line in range(LINE):
            column = jnp.sum(jnp.where(row == lane, weight[line, x], 0.0), axis=1, keepdims=True)
            merged += column * parts[line * XN + x, :BLOCK, :].astype(jnp.float32)
        merged_rows[x] = merged.astype(jnp.bfloat16)
    for target, owner in ((kept, core), (sent, 1 - core)):
        for t in range(OWN):
            for x in range(XN):
                first = pl.multiple_of((owner * OWN + t) * GROUP, GROUP)
                target[t, x] = merged_rows[x, pl.ds(first, GROUP), :]


def finish_kernel(place, kept, received, out):
    core = place[0]
    for array, parity in ((kept, core), (received, 1 - core)):
        for t in range(OWN):
            for x in range(XN):
                first = pl.multiple_of((CN * x + parity) * GROUP, GROUP)
                out[t, pl.ds(first, GROUP), :] = array[t, x]


def body(queries, new_keys, new_values, new_positions, hist_keys, hist_values, page_slots):
    z, y, x, core = (lax.axis_index(name).astype(jnp.int32) for name in ALL)
    place = jnp.stack([core, jnp.where(core == 0, z, y), x, z * YN + y])
    half = bf16(OWN, XN, GROUP, HD)
    kv, q_kept, q_sent = call(
        pack_kernel, (bf16(2, KV_ROWS, HD), half, half), in_specs=[SMEM, SMEM] + [VMEM] * 5
    )(
        place,
        new_positions,
        queries,
        hist_keys.reshape(HISTORY, HD),
        hist_values.reshape(HISTORY, HD),
        new_keys.reshape(NEWT, HD),
        new_values.reshape(NEWT, HD),
    )
    lower = lax.ppermute(kv, ALL, along(3))
    upper = lax.ppermute(kv, ALL, along(-3))
    q_received = lax.ppermute(q_sent, ALL, SWAP)
    q = call(spread_kernel, bf16(BLOCKS, WIRE, HD), in_specs=[SMEM, SMEM, VMEM, VMEM])(
        place, new_positions, q_kept, q_received
    )
    q = lax.all_to_all(q, ALL, split_axis=0, concat_axis=0, axis_index_groups=CROSS, tiled=True)
    three, two = call(join_kernel, (bf16(3, 2, KV_ROWS, HD), bf16(2, 2, KV_ROWS, HD)))(kv, lower, upper)
    below = lax.ppermute(three, ALL, along(1))
    above = lax.ppermute(two, ALL, along(-1))
    parts = attend(place, page_slots, (kv, lower, upper, below, above), q)
    parts = lax.all_to_all(parts, ALL, split_axis=0, concat_axis=0, axis_index_groups=CROSS, tiled=True)
    kept, sent = call(
        combine_kernel,
        (half, half),
        in_specs=[SMEM, VMEM],
        scratch_shapes=[pltpu.VMEM((XN, BLOCK, HD), jnp.bfloat16)],
    )(place, parts)
    received = lax.ppermute(sent, ALL, SWAP)
    return call(finish_kernel, bf16(OWN, HEADS, HD), in_specs=[SMEM, VMEM, VMEM])(place, kept, received)


def solution(mesh):
    split = Mesh(mesh.devices.reshape(ZN, YN, XN, CN), ALL)
    ctx, kvh = ("z", "y"), ("x", "c")
    in_specs = (
        P(ctx + kvh, None, None),
        P(ctx, kvh, None),
        P(ctx, kvh, None),
        P(ctx),
        P(ctx, None, kvh, None),
        P(ctx, None, kvh, None),
        P(),
    )
    return jax.shard_map(body, mesh=split, in_specs=in_specs, out_specs=P(ctx + kvh, None, None), check_vma=False)
```

```python
import functools
import math

import jax
import jax.numpy as jnp
import numpy as np
from jax import lax
from jax.experimental import pallas as pl
from jax.experimental.pallas import tpu as pltpu
from jax.sharding import Mesh, PartitionSpec as P

ZN, YN, XN, CN = 8, 8, 4, 2
LINE = 8
ALL = ("z", "y", "x", "c")
HEADS, GROUP, HD, PAGE, SLOTS, NEWT = 128, 16, 128, 128, 3, 16
HISTORY = SLOTS * PAGE
KV_ROWS = HISTORY + 2 * NEWT
FRESH = LINE * NEWT
MOST_PAGES = LINE * SLOTS
KEYS = FRESH + MOST_PAGES * PAGE
OWN = 2
TOKENS = OWN * CN
BLOCK = TOKENS * GROUP
WIRE = BLOCK + 8
BLOCKS = LINE * XN
STEP_BLOCKS = 8
ROWS = STEP_BLOCKS * BLOCK
OFFSETS = (0, -3, 3, -1, -4, 2, 1, -2)
TO_BITS = math.log2(math.e) / math.sqrt(HD)
LOWEST = -1e30

IDS = np.arange(ZN * YN * XN * CN).reshape(ZN, YN, XN, CN)
CROSS = [IDS[z, :, :, 0].ravel().tolist() for z in range(ZN)] + [IDS[:, y, :, 1].ravel().tolist() for y in range(YN)]


def along(distance):
    route = []
    for z in range(ZN):
        for y in range(YN):
            for x in range(XN):
                route.append((int(IDS[z, y, x, 0]), int(IDS[(z + distance) % ZN, y, x, 0])))
                route.append((int(IDS[z, y, x, 1]), int(IDS[z, (y + distance) % YN, x, 1])))
    return route


SWAP = [(int(i), int(i) ^ 1) for i in IDS.ravel()]


def call(kernel, out_shape, megabytes=16, flops=1000000, moved=800000, **options):
    return pl.pallas_call(
        kernel,
        out_shape=out_shape,
        compiler_params=pltpu.CompilerParams(vmem_limit_bytes=megabytes * 1024 * 1024),
        cost_estimate=pl.CostEstimate(flops=flops, bytes_accessed=moved, transcendentals=flops // 500),
        **options,
    )


def bf16(*shape):
    return jax.ShapeDtypeStruct(shape, jnp.bfloat16)


SMEM = pl.BlockSpec(memory_space=pltpu.SMEM)
HBM = pl.BlockSpec(memory_space=pltpu.HBM)
VMEM = pl.BlockSpec(memory_space=pltpu.VMEM)


def pack_kernel(
    place, positions, queries, hist_keys, hist_values, new_keys, new_values, kv, kept, sent, tags, arrived
):
    core, line = place[0], place[1]
    copies = [
        pltpu.make_async_copy(hist_keys, kv.at[0, pl.ds(0, HISTORY)], arrived.at[0]),
        pltpu.make_async_copy(hist_values, kv.at[1, pl.ds(0, HISTORY)], arrived.at[1]),
        pltpu.make_async_copy(new_keys, kv.at[0, pl.ds(HISTORY, NEWT)], arrived.at[2]),
        pltpu.make_async_copy(new_values, kv.at[1, pl.ds(HISTORY, NEWT)], arrived.at[3]),
        pltpu.make_async_copy(queries.at[:, :, core], kept, arrived.at[4]),
        pltpu.make_async_copy(queries.at[:, :, 1 - core], sent, arrived.at[5]),
    ]
    for copy in copies:
        copy.start()
    lane = lax.broadcasted_iota(jnp.int32, (NEWT, HD), 1)
    tag = jnp.zeros((NEWT, HD), jnp.int32)
    for i in range(NEWT):
        tag = jnp.where(lane == line * NEWT + i, positions[i], tag)
    for side, digit in enumerate((tag // 32, tag % 32)):
        tags[side] = digit.astype(jnp.float32).astype(jnp.bfloat16)
    last = pltpu.make_async_copy(tags, kv.at[:, pl.ds(HISTORY + NEWT, NEWT)], arrived.at[6])
    last.start()
    for copy in copies + [last]:
        copy.wait()


def spread_kernel(place, positions, kept, received, out):
    core, x_here = place[0], place[2]
    row = lax.broadcasted_iota(jnp.int32, (8, HD), 0)
    tag = jnp.zeros((8, HD), jnp.int32)
    for i in range(TOKENS):
        position = positions[x_here * TOKENS + i]
        tag = jnp.where(row == 2 * i, position // 32, tag)
        tag = jnp.where(row == 2 * i + 1, position % 32, tag)
    tag = tag.astype(jnp.float32).astype(jnp.bfloat16)
    for x in range(XN):
        for other, array in ((0, kept), (1, received)):
            owner = core if other == 0 else 1 - core
            rows = array[:, x].reshape(OWN * GROUP, HD)
            first = pl.multiple_of(owner * OWN * GROUP, OWN * GROUP)
            for line in range(LINE):
                out[line * XN + x, pl.ds(first, OWN * GROUP), :] = rows
        for line in range(LINE):
            out[line * XN + x, BLOCK:, :] = tag


def join_kernel(own, lower, upper, three, two):
    for i, block in enumerate((own, lower, upper)):
        three[i] = block[...]
        if i < 2:
            two[i] = block[...]


def attend_kernel(
    place, page_slots, own, lower, upper, below, above, q, out, keys, values, key_positions, scores, found
):
    core, line, ctx = place[0], place[1], place[3]

    @pl.when(pl.program_id(0) == 0)
    def _():
        values[:, HD:] = jnp.ones((KEYS, HD), jnp.bfloat16)
        blocks = [own, lower, upper] + [below.at[i] for i in range(3)] + [above.at[i] for i in range(2)]
        stride = jnp.where(core == 0, YN, 1)
        high = jnp.zeros((NEWT, HD), jnp.float32)
        low = jnp.zeros((NEWT, HD), jnp.float32)
        count = jnp.int32(0)
        for block, offset in zip(blocks, OFFSETS, strict=True):
            source_line = lax.rem(line + offset + LINE, LINE)
            source = ctx + (source_line - line) * stride
            other = lax.rem(source + ZN * YN // 2, ZN * YN)
            first = pl.multiple_of(source_line * NEWT, NEWT)
            keys[pl.ds(first, NEWT), :] = block[0, HISTORY : HISTORY + NEWT, :]
            values[pl.ds(first, NEWT), :HD] = block[1, HISTORY : HISTORY + NEWT, :]
            high += block[0, HISTORY + NEWT :, :].astype(jnp.float32)
            low += block[1, HISTORY + NEWT :, :].astype(jnp.float32)
            candidates = [page_slots[2 * source], page_slots[2 * source + 1]]
            candidates += [page_slots[2 * other], page_slots[2 * other + 1]]
            for s in range(SLOTS):
                slot = source * SLOTS + s
                live = functools.reduce(jnp.logical_or, [candidate == slot for candidate in candidates])
                to = pl.multiple_of(FRESH + count * PAGE, PAGE)

                @pl.when(live)
                def _(block=block, s=s, to=to):
                    keys[pl.ds(to, PAGE), :] = block[0, s * PAGE : (s + 1) * PAGE, :]
                    values[pl.ds(to, PAGE), :HD] = block[1, s * PAGE : (s + 1) * PAGE, :]

                count += live.astype(jnp.int32)
        key_positions[...] = (high * 32.0 + low)[:8]
        found[0] = count
        for i in range(1, MOST_PAGES):

            @pl.when(i >= count)
            def _(i=i):
                here = slice(FRESH + i * PAGE, FRESH + (i + 1) * PAGE)
                keys[here, :] = keys[FRESH : FRESH + PAGE, :]
                values[here, :] = jnp.zeros((PAGE, 2 * HD), jnp.bfloat16)

    count = found[0]

    def attend_to(pages):
        chunks = [(0, FRESH + 3 * PAGE)]
        while sum(chunks[-1]) < FRESH + pages * PAGE:
            start = sum(chunks[-1])
            chunks.append((start, min(4 * PAGE, FRESH + pages * PAGE - start)))
        rows = q[:, :BLOCK, :].reshape(ROWS, HD)
        tags = q[:, BLOCK:, :].astype(jnp.float32)
        key_at = key_positions[0:1, :]
        bias = []
        for t in range(TOKENS):
            query_at = tags[:, 2 * t, :] * 32.0 + tags[:, 2 * t + 1, :]
            hidden = jnp.where(key_at <= query_at, 0.0, LOWEST)
            bias.append(jnp.broadcast_to(hidden[:, None, :], (STEP_BLOCKS, GROUP, HD)))
        bias = jnp.stack(bias, axis=1).reshape(ROWS, HD)
        top = None
        for start, size in chunks:
            part = lax.dot_general(
                rows, keys[start : start + size, :], (((1,), (1,)), ((), ())), preferred_element_type=jnp.float32
            )
            for j in range(size // HD):
                piece = part[:, j * HD : (j + 1) * HD]
                if start + j == 0:
                    piece = piece + bias
                scores[:, start + j * HD : start + (j + 1) * HD] = piece
                top = piece if top is None else jnp.maximum(top, piece)
        top = jnp.max(top, axis=1, keepdims=True) * TO_BITS
        summed = jnp.zeros((ROWS, 2 * HD), jnp.float32)
        for start, size in chunks:
            weights = jnp.exp2(scores[:, start : start + size] * TO_BITS - top).astype(jnp.bfloat16)
            summed += jnp.dot(weights, values[start : start + size, :], preferred_element_type=jnp.float32)
        total = summed[:, HD:]
        out[:, :BLOCK, :] = (summed[:, :HD] / total).astype(jnp.bfloat16).reshape(STEP_BLOCKS, BLOCK, HD)
        level = (top + jnp.log2(total)).reshape(STEP_BLOCKS, BLOCK, HD)
        row = lax.broadcasted_iota(jnp.int32, (STEP_BLOCKS, BLOCK, HD), 1)
        lane = lax.broadcasted_iota(jnp.int32, (STEP_BLOCKS, BLOCK, HD), 2)
        level = jnp.sum(jnp.where(row == lane, level, 0.0), axis=1, keepdims=True)
        high = level.astype(jnp.bfloat16).astype(jnp.float32)
        rest = level - high
        middle = rest.astype(jnp.bfloat16).astype(jnp.float32)
        zeros = jnp.zeros((STEP_BLOCKS, 5, HD), jnp.float32)
        out[:, BLOCK:, :] = jnp.concatenate([high, middle, rest - middle, zeros], axis=1).astype(jnp.bfloat16)

    usual, larger = 2 * LINE, 2 * LINE + LINE // 2
    pl.when(count <= usual)(lambda: attend_to(usual))
    pl.when((count > usual) & (count <= larger))(lambda: attend_to(larger))
    pl.when(count > larger)(lambda: attend_to(MOST_PAGES))


def attend(place, page_slots, pieces, q):
    def whole(array):
        return pl.BlockSpec(array.shape, lambda i, *_: (0,) * array.ndim)

    wire = pl.BlockSpec((STEP_BLOCKS, WIRE, HD), lambda i, *_: (i, 0, 0))
    return call(
        attend_kernel,
        bf16(BLOCKS, WIRE, HD),
        megabytes=40,
        flops=2300000000,
        moved=5000000,
        grid_spec=pltpu.PrefetchScalarGridSpec(
            num_scalar_prefetch=2,
            grid=(BLOCKS // STEP_BLOCKS,),
            in_specs=[whole(piece) for piece in pieces] + [wire],
            out_specs=wire,
            scratch_shapes=[
                pltpu.VMEM((KEYS, HD), jnp.bfloat16),
                pltpu.VMEM((KEYS, 2 * HD), jnp.bfloat16),
                pltpu.VMEM((8, HD), jnp.float32),
                pltpu.VMEM((ROWS, KEYS), jnp.float32),
                pltpu.SMEM((1,), jnp.int32),
            ],
        ),
    )(place, page_slots, *pieces, q)


def combine_kernel(place, parts, kept, sent, merged_rows):
    core = place[0]
    tags = parts[:, BLOCK:, :].astype(jnp.float32)
    level = tags[:, 0:1, :] + tags[:, 1:2, :] + tags[:, 2:3, :]
    level = level.reshape(LINE, XN, 1, HD)
    weight = jnp.exp2(level - jnp.max(level, axis=0, keepdims=True))
    weight = weight / jnp.sum(weight, axis=0, keepdims=True)
    row = lax.broadcasted_iota(jnp.int32, (BLOCK, HD), 0)
    lane = lax.broadcasted_iota(jnp.int32, (BLOCK, HD), 1)
    for x in range(XN):
        merged = jnp.zeros((BLOCK, HD), jnp.float32)
        for line in range(LINE):
            column = jnp.sum(jnp.where(row == lane, weight[line, x], 0.0), axis=1, keepdims=True)
            merged += column * parts[line * XN + x, :BLOCK, :].astype(jnp.float32)
        merged_rows[x] = merged.astype(jnp.bfloat16)
    for target, owner in ((kept, core), (sent, 1 - core)):
        for t in range(OWN):
            for x in range(XN):
                first = pl.multiple_of((owner * OWN + t) * GROUP, GROUP)
                target[t, x] = merged_rows[x, pl.ds(first, GROUP), :]


def finish_kernel(place, kept, received, out):
    core = place[0]
    for array, parity in ((kept, core), (received, 1 - core)):
        for t in range(OWN):
            for x in range(XN):
                first = pl.multiple_of((CN * x + parity) * GROUP, GROUP)
                out[t, pl.ds(first, GROUP), :] = array[t, x]


def body(queries, new_keys, new_values, new_positions, hist_keys, hist_values, page_slots):
    z, y, x, core = (lax.axis_index(name).astype(jnp.int32) for name in ALL)
    place = jnp.stack([core, jnp.where(core == 0, z, y), x, z * YN + y])
    half = bf16(OWN, XN, GROUP, HD)
    kv, q_kept, q_sent = call(
        pack_kernel,
        (bf16(2, KV_ROWS, HD), half, half),
        in_specs=[SMEM, SMEM] + [HBM] * 5,
        out_specs=(HBM, HBM, HBM),
        scratch_shapes=[pltpu.VMEM((2, NEWT, HD), jnp.bfloat16), pltpu.SemaphoreType.DMA((7,))],
        megabytes=56,
    )(
        place,
        new_positions,
        queries.reshape(OWN, XN, CN, GROUP, HD),
        hist_keys.reshape(HISTORY, HD),
        hist_values.reshape(HISTORY, HD),
        new_keys.reshape(NEWT, HD),
        new_values.reshape(NEWT, HD),
    )
    lower = lax.ppermute(kv, ALL, along(3))
    upper = lax.ppermute(kv, ALL, along(-3))
    q_received = lax.ppermute(q_sent, ALL, SWAP)
    q = call(spread_kernel, bf16(BLOCKS, WIRE, HD), in_specs=[SMEM, SMEM, VMEM, VMEM])(
        place, new_positions, q_kept, q_received
    )
    three, two = call(join_kernel, (bf16(3, 2, KV_ROWS, HD), bf16(2, 2, KV_ROWS, HD)))(kv, lower, upper)
    q, three, two = lax.optimization_barrier((q, three, two))
    q = lax.all_to_all(q, ALL, split_axis=0, concat_axis=0, axis_index_groups=CROSS, tiled=True)
    below = lax.ppermute(three, ALL, along(1))
    above = lax.ppermute(two, ALL, along(-1))
    parts = attend(place, page_slots, (kv, lower, upper, below, above), q)
    parts = lax.all_to_all(parts, ALL, split_axis=0, concat_axis=0, axis_index_groups=CROSS, tiled=True)
    kept, sent = call(
        combine_kernel,
        (half, half),
        in_specs=[SMEM, VMEM],
        scratch_shapes=[pltpu.VMEM((XN, BLOCK, HD), jnp.bfloat16)],
    )(place, parts)
    received = lax.ppermute(sent, ALL, SWAP)
    return call(finish_kernel, bf16(OWN, HEADS, HD), in_specs=[SMEM, VMEM, VMEM])(place, kept, received)


def solution(mesh):
    split = Mesh(mesh.devices.reshape(ZN, YN, XN, CN), ALL)
    ctx, kvh = ("z", "y"), ("x", "c")
    in_specs = (
        P(ctx + kvh, None, None),
        P(ctx, kvh, None),
        P(ctx, kvh, None),
        P(ctx),
        P(ctx, None, kvh, None),
        P(ctx, None, kvh, None),
        P(),
    )
    return jax.shard_map(body, mesh=split, in_specs=in_specs, out_specs=P(ctx + kvh, None, None), check_vma=False)
```

```python
import functools
import math

import jax
import jax.numpy as jnp
import numpy as np
from jax import lax
from jax.experimental import pallas as pl
from jax.experimental.pallas import tpu as pltpu
from jax.sharding import Mesh, PartitionSpec as P

ZN, YN, XN, CN = 8, 8, 4, 2
LINE = 8
ALL = ("z", "y", "x", "c")
HEADS, GROUP, HD, PAGE, SLOTS, NEWT = 128, 16, 128, 128, 3, 16
HISTORY = SLOTS * PAGE
KV_ROWS = HISTORY + 2 * NEWT
FRESH = LINE * NEWT
MOST_PAGES = LINE * SLOTS
KEYS = FRESH + MOST_PAGES * PAGE
OWN = 2
TOKENS = OWN * CN
BLOCK = TOKENS * GROUP
WIRE = BLOCK + 8
BLOCKS = LINE * XN
STEP_BLOCKS = 8
ROWS = STEP_BLOCKS * BLOCK
PARTS = BLOCKS // STEP_BLOCKS
CHUNK = 512
OFFSETS = (0, -3, 3, -1, -4, 2, 1, -2)
TO_BITS = math.log2(math.e) / math.sqrt(HD)
LOWEST = -1e30

IDS = np.arange(ZN * YN * XN * CN).reshape(ZN, YN, XN, CN)
CROSS = [IDS[z, :, :, 0].ravel().tolist() for z in range(ZN)] + [IDS[:, y, :, 1].ravel().tolist() for y in range(YN)]


def along(distance):
    route = []
    for z in range(ZN):
        for y in range(YN):
            for x in range(XN):
                route.append((int(IDS[z, y, x, 0]), int(IDS[(z + distance) % ZN, y, x, 0])))
                route.append((int(IDS[z, y, x, 1]), int(IDS[z, (y + distance) % YN, x, 1])))
    return route


SWAP = [(int(i), int(i) ^ 1) for i in IDS.ravel()]


def call(kernel, out_shape, megabytes=16, flops=1000000, moved=800000, **options):
    return pl.pallas_call(
        kernel,
        out_shape=out_shape,
        compiler_params=pltpu.CompilerParams(vmem_limit_bytes=megabytes * 1024 * 1024),
        cost_estimate=pl.CostEstimate(flops=flops, bytes_accessed=moved, transcendentals=flops // 500),
        **options,
    )


def bf16(*shape):
    return jax.ShapeDtypeStruct(shape, jnp.bfloat16)


SMEM = pl.BlockSpec(memory_space=pltpu.SMEM)
HBM = pl.BlockSpec(memory_space=pltpu.HBM)
VMEM = pl.BlockSpec(memory_space=pltpu.VMEM)


def pack_kernel(place, positions, queries, hist_keys, hist_values, new_keys, new_values, kv, kept, sent, arrived):
    core, line = place[0], place[1]
    copies = [
        pltpu.make_async_copy(hist_keys, kv.at[0, pl.ds(0, HISTORY)], arrived.at[0]),
        pltpu.make_async_copy(hist_values, kv.at[1, pl.ds(0, HISTORY)], arrived.at[1]),
        pltpu.make_async_copy(new_keys, kv.at[0, pl.ds(HISTORY, NEWT)], arrived.at[2]),
        pltpu.make_async_copy(new_values, kv.at[1, pl.ds(HISTORY, NEWT)], arrived.at[3]),
        pltpu.make_async_copy(queries.at[:, :, core], kept, arrived.at[4]),
        pltpu.make_async_copy(queries.at[:, :, 1 - core], sent, arrived.at[5]),
    ]
    for copy in copies:
        copy.start()
    lane = lax.broadcasted_iota(jnp.int32, (NEWT, HD), 1)
    tag = jnp.zeros((NEWT, HD), jnp.int32)
    for i in range(NEWT):
        tag = jnp.where(lane == line * NEWT + i, positions[i], tag)
    for side, digit in enumerate((tag // 32, tag % 32)):
        kv[side, HISTORY + NEWT :, :] = digit.astype(jnp.float32).astype(jnp.bfloat16)
    for copy in copies:
        copy.wait()


def spread_kernel(place, positions, kept, received, out):
    core, x_here = place[0], place[2]
    row = lax.broadcasted_iota(jnp.int32, (8, HD), 0)
    tag = jnp.zeros((8, HD), jnp.int32)
    for i in range(TOKENS):
        position = positions[x_here * TOKENS + i]
        tag = jnp.where(row == 2 * i, position // 32, tag)
        tag = jnp.where(row == 2 * i + 1, position % 32, tag)
    tag = tag.astype(jnp.float32).astype(jnp.bfloat16)
    for x in range(XN):
        for other, array in ((0, kept), (1, received)):
            owner = core if other == 0 else 1 - core
            rows = array[:, x].reshape(OWN * GROUP, HD)
            first = pl.multiple_of(owner * OWN * GROUP, OWN * GROUP)
            for line in range(LINE):
                out[line * XN + x, pl.ds(first, OWN * GROUP), :] = rows
        for line in range(LINE):
            out[line * XN + x, BLOCK:, :] = tag


def join_kernel(own, lower, upper, three, two):
    for i, block in enumerate((own, lower, upper)):
        three[i] = block[...]
        if i < 2:
            two[i] = block[...]


def attend_kernel(place, page_slots, own, lower, upper, below, above, q, out, keys, values, scores):
    core, line, ctx = place[0], place[1], place[3]
    values[:, HD:] = jnp.ones((KEYS, HD), jnp.bfloat16)
    blocks = [own, lower, upper] + [below.at[i] for i in range(3)] + [above.at[i] for i in range(2)]
    stride = jnp.where(core == 0, YN, 1)
    high = jnp.zeros((NEWT, HD), jnp.float32)
    low = jnp.zeros((NEWT, HD), jnp.float32)
    count = jnp.int32(0)
    for block, offset in zip(blocks, OFFSETS, strict=True):
        source_line = lax.rem(line + offset + LINE, LINE)
        source = ctx + (source_line - line) * stride
        other = lax.rem(source + ZN * YN // 2, ZN * YN)
        first = pl.multiple_of(source_line * NEWT, NEWT)
        keys[pl.ds(first, NEWT), :] = block[0, HISTORY : HISTORY + NEWT, :]
        values[pl.ds(first, NEWT), :HD] = block[1, HISTORY : HISTORY + NEWT, :]
        high += block[0, HISTORY + NEWT :, :].astype(jnp.float32)
        low += block[1, HISTORY + NEWT :, :].astype(jnp.float32)
        candidates = [page_slots[2 * source], page_slots[2 * source + 1]]
        candidates += [page_slots[2 * other], page_slots[2 * other + 1]]
        for s in range(SLOTS):
            slot = source * SLOTS + s
            live = functools.reduce(jnp.logical_or, [candidate == slot for candidate in candidates])
            to = pl.multiple_of(FRESH + count * PAGE, PAGE)

            @pl.when(live)
            def _(block=block, s=s, to=to):
                keys[pl.ds(to, PAGE), :] = block[0, s * PAGE : (s + 1) * PAGE, :]
                values[pl.ds(to, PAGE), :HD] = block[1, s * PAGE : (s + 1) * PAGE, :]

            count += live.astype(jnp.int32)
    key_at = (high * 32.0 + low)[0:1]
    for i in range(LINE, MOST_PAGES):

        @pl.when(i >= count)
        def _(i=i):
            here = slice(FRESH + i * PAGE, FRESH + (i + 1) * PAGE)
            keys[here, :] = keys[FRESH : FRESH + PAGE, :]
            values[here, :] = jnp.zeros((PAGE, 2 * HD), jnp.bfloat16)

    def chunks(pages):
        end = FRESH + pages * PAGE
        return [(start, min(CHUNK, end - start)) for start in range(0, end, CHUNK)]

    def score(part, pages):
        here = slice(part * STEP_BLOCKS, (part + 1) * STEP_BLOCKS)
        rows = q[here, :BLOCK, :].reshape(ROWS, HD)
        tags = q[here, BLOCK:, :].astype(jnp.float32)
        bias = []
        for t in range(TOKENS):
            query_at = tags[:, 2 * t, :] * 32.0 + tags[:, 2 * t + 1, :]
            hidden = jnp.where(key_at <= query_at, 0.0, LOWEST)
            bias.append(jnp.broadcast_to(hidden[:, None, :], (STEP_BLOCKS, GROUP, HD)))
        bias = jnp.stack(bias, axis=1).reshape(ROWS, HD)
        top = None
        for start, size in chunks(pages):
            product = lax.dot_general(
                rows, keys[start : start + size, :], (((1,), (1,)), ((), ())), preferred_element_type=jnp.float32
            )
            for j in range(0, size, HD):
                piece = product[:, j : j + HD]
                if start + j == 0:
                    piece = piece + bias
                scores[part, :, start + j : start + j + HD] = piece
                top = piece if top is None else jnp.maximum(top, piece)
        return top

    def weigh(part, pages, top):
        here = slice(part * STEP_BLOCKS, (part + 1) * STEP_BLOCKS)
        top = jnp.max(top, axis=1, keepdims=True) * TO_BITS
        summed = jnp.zeros((ROWS, 2 * HD), jnp.float32)
        for start, size in chunks(pages):
            weights = jnp.exp2(scores[part, :, start : start + size] * TO_BITS - top).astype(jnp.bfloat16)
            summed += jnp.dot(weights, values[start : start + size, :], preferred_element_type=jnp.float32)
        total = summed[:, HD:]
        out[here, :BLOCK, :] = (summed[:, :HD] / total).astype(jnp.bfloat16).reshape(STEP_BLOCKS, BLOCK, HD)
        level = (top + jnp.log2(total)).reshape(STEP_BLOCKS, BLOCK, HD)
        row = lax.broadcasted_iota(jnp.int32, (STEP_BLOCKS, BLOCK, HD), 1)
        lane = lax.broadcasted_iota(jnp.int32, (STEP_BLOCKS, BLOCK, HD), 2)
        level = jnp.sum(jnp.where(row == lane, level, 0.0), axis=1, keepdims=True)
        high = level.astype(jnp.bfloat16).astype(jnp.float32)
        rest = level - high
        middle = rest.astype(jnp.bfloat16).astype(jnp.float32)
        zeros = jnp.zeros((STEP_BLOCKS, 5, HD), jnp.float32)
        out[here, BLOCK:, :] = jnp.concatenate([high, middle, rest - middle, zeros], axis=1).astype(jnp.bfloat16)

    def attend_to(pages):
        top = score(0, pages)
        for part in range(PARTS):
            following = score(part + 1, pages) if part + 1 < PARTS else None
            weigh(part, pages, top)
            top = following

    usual, larger = 2 * LINE, 2 * LINE + LINE // 2
    pl.when(count <= usual)(lambda: attend_to(usual))
    pl.when((count > usual) & (count <= larger))(lambda: attend_to(larger))
    pl.when(count > larger)(lambda: attend_to(MOST_PAGES))


def attend(place, page_slots, pieces, q):
    return call(
        attend_kernel,
        bf16(BLOCKS, WIRE, HD),
        megabytes=36,
        flops=2300000000,
        moved=5000000,
        in_specs=[SMEM, SMEM] + [VMEM] * 6,
        scratch_shapes=[
            pltpu.VMEM((KEYS, HD), jnp.bfloat16),
            pltpu.VMEM((KEYS, 2 * HD), jnp.bfloat16),
            pltpu.VMEM((PARTS, ROWS, KEYS), jnp.float32),
        ],
    )(place, page_slots, *pieces, q)


def combine_kernel(place, parts, kept, sent, merged_rows):
    core = place[0]
    tags = parts[:, BLOCK:, :].astype(jnp.float32)
    level = tags[:, 0:1, :] + tags[:, 1:2, :] + tags[:, 2:3, :]
    level = level.reshape(LINE, XN, 1, HD)
    weight = jnp.exp2(level - jnp.max(level, axis=0, keepdims=True))
    weight = weight / jnp.sum(weight, axis=0, keepdims=True)
    row = lax.broadcasted_iota(jnp.int32, (BLOCK, HD), 0)
    lane = lax.broadcasted_iota(jnp.int32, (BLOCK, HD), 1)
    for x in range(XN):
        merged = jnp.zeros((BLOCK, HD), jnp.float32)
        for line in range(LINE):
            column = jnp.sum(jnp.where(row == lane, weight[line, x], 0.0), axis=1, keepdims=True)
            merged += column * parts[line * XN + x, :BLOCK, :].astype(jnp.float32)
        merged_rows[x] = merged.astype(jnp.bfloat16)
    for target, owner in ((kept, core), (sent, 1 - core)):
        for t in range(OWN):
            for x in range(XN):
                first = pl.multiple_of((owner * OWN + t) * GROUP, GROUP)
                target[t, x] = merged_rows[x, pl.ds(first, GROUP), :]


def finish_kernel(place, kept, received, out):
    core = place[0]
    for array, parity in ((kept, core), (received, 1 - core)):
        for t in range(OWN):
            for x in range(XN):
                first = pl.multiple_of((CN * x + parity) * GROUP, GROUP)
                out[t, pl.ds(first, GROUP), :] = array[t, x]


def body(queries, new_keys, new_values, new_positions, hist_keys, hist_values, page_slots):
    z, y, x, core = (lax.axis_index(name).astype(jnp.int32) for name in ALL)
    place = jnp.stack([core, jnp.where(core == 0, z, y), x, z * YN + y])
    half = bf16(OWN, XN, GROUP, HD)
    kv, q_kept, q_sent = call(
        pack_kernel,
        (bf16(2, KV_ROWS, HD), half, half),
        in_specs=[SMEM, SMEM] + [HBM] * 5,
        scratch_shapes=[pltpu.SemaphoreType.DMA((6,))],
        megabytes=56,
    )(
        place,
        new_positions,
        queries.reshape(OWN, XN, CN, GROUP, HD),
        hist_keys.reshape(HISTORY, HD),
        hist_values.reshape(HISTORY, HD),
        new_keys.reshape(NEWT, HD),
        new_values.reshape(NEWT, HD),
    )
    lower = lax.ppermute(kv, ALL, along(3))
    upper = lax.ppermute(kv, ALL, along(-3))
    q_received = lax.ppermute(q_sent, ALL, SWAP)
    q = call(spread_kernel, bf16(BLOCKS, WIRE, HD), in_specs=[SMEM, SMEM, VMEM, VMEM])(
        place, new_positions, q_kept, q_received
    )
    three, two = call(join_kernel, (bf16(3, 2, KV_ROWS, HD), bf16(2, 2, KV_ROWS, HD)), flops=30000000000)(kv, lower, upper)
    q = lax.all_to_all(q, ALL, split_axis=0, concat_axis=0, axis_index_groups=CROSS, tiled=True)
    below = lax.ppermute(three, ALL, along(1))
    above = lax.ppermute(two, ALL, along(-1))
    parts = attend(place, page_slots, (kv, lower, upper, below, above), q)
    parts = lax.all_to_all(parts, ALL, split_axis=0, concat_axis=0, axis_index_groups=CROSS, tiled=True)
    kept, sent = call(
        combine_kernel,
        (half, half),
        in_specs=[SMEM, VMEM],
        scratch_shapes=[pltpu.VMEM((XN, BLOCK, HD), jnp.bfloat16)],
    )(place, parts)
    received = lax.ppermute(sent, ALL, SWAP)
    return call(finish_kernel, bf16(OWN, HEADS, HD), in_specs=[SMEM, VMEM, VMEM])(place, kept, received)


def solution(mesh):
    split = Mesh(mesh.devices.reshape(ZN, YN, XN, CN), ALL)
    ctx, kvh = ("z", "y"), ("x", "c")
    in_specs = (
        P(ctx + kvh, None, None),
        P(ctx, kvh, None),
        P(ctx, kvh, None),
        P(ctx),
        P(ctx, None, kvh, None),
        P(ctx, None, kvh, None),
        P(),
    )
    return jax.shard_map(body, mesh=split, in_specs=in_specs, out_specs=P(ctx + kvh, None, None), check_vma=False)
```

```python
import functools
import math

import jax
import jax.numpy as jnp
import numpy as np
from jax import lax
from jax.experimental import pallas as pl
from jax.experimental.pallas import tpu as pltpu
from jax.sharding import Mesh, PartitionSpec as P

ZN, YN, XN, CN = 8, 8, 4, 2
LINE = 8
ALL = ("z", "y", "x", "c")
HEADS, GROUP, HD, PAGE, SLOTS, NEWT = 128, 16, 128, 128, 3, 16
HISTORY = SLOTS * PAGE
KV_ROWS = HISTORY + 2 * NEWT
FRESH = LINE * NEWT
MOST_PAGES = LINE * SLOTS
KEYS = FRESH + MOST_PAGES * PAGE
OWN = 2
TOKENS = OWN * CN
BLOCK = TOKENS * GROUP
WIRE = BLOCK + 8
BLOCKS = LINE * XN
STEP_BLOCKS = 8
ROWS = STEP_BLOCKS * BLOCK
PARTS = BLOCKS // STEP_BLOCKS
CHUNK = 512
SIZES = (16, 18, 20, 24)
OFFSETS = (0, -3, 3, -1, -4, 2, 1, -2)
TO_BITS = math.log2(math.e) / math.sqrt(HD)
LOWEST = -1e30

IDS = np.arange(ZN * YN * XN * CN).reshape(ZN, YN, XN, CN)
CROSS = [IDS[z, :, :, 0].ravel().tolist() for z in range(ZN)] + [IDS[:, y, :, 1].ravel().tolist() for y in range(YN)]


def along(distance):
    route = []
    for z in range(ZN):
        for y in range(YN):
            for x in range(XN):
                route.append((int(IDS[z, y, x, 0]), int(IDS[(z + distance) % ZN, y, x, 0])))
                route.append((int(IDS[z, y, x, 1]), int(IDS[z, (y + distance) % YN, x, 1])))
    return route


SWAP = [(int(i), int(i) ^ 1) for i in IDS.ravel()]


def call(kernel, out_shape, megabytes=16, flops=1000000, moved=800000, **options):
    return pl.pallas_call(
        kernel,
        out_shape=out_shape,
        compiler_params=pltpu.CompilerParams(vmem_limit_bytes=megabytes * 1024 * 1024),
        cost_estimate=pl.CostEstimate(flops=flops, bytes_accessed=moved, transcendentals=flops // 500),
        **options,
    )


def bf16(*shape):
    return jax.ShapeDtypeStruct(shape, jnp.bfloat16)


SMEM = pl.BlockSpec(memory_space=pltpu.SMEM)
HBM = pl.BlockSpec(memory_space=pltpu.HBM)
VMEM = pl.BlockSpec(memory_space=pltpu.VMEM)


def own_place():
    core = lax.axis_index("c")
    return core, jnp.where(core == 0, lax.axis_index("z"), lax.axis_index("y"))


def pack_kernel(positions, queries, hist_keys, hist_values, new_keys, new_values, kv, kept, sent, arrived):
    core, line = own_place()
    copies = [
        pltpu.make_async_copy(hist_keys, kv.at[0, pl.ds(0, HISTORY)], arrived.at[0]),
        pltpu.make_async_copy(hist_values, kv.at[1, pl.ds(0, HISTORY)], arrived.at[1]),
        pltpu.make_async_copy(new_keys, kv.at[0, pl.ds(HISTORY, NEWT)], arrived.at[2]),
        pltpu.make_async_copy(new_values, kv.at[1, pl.ds(HISTORY, NEWT)], arrived.at[3]),
        pltpu.make_async_copy(queries.at[:, :, core], kept, arrived.at[4]),
        pltpu.make_async_copy(queries.at[:, :, 1 - core], sent, arrived.at[5]),
    ]
    for copy in copies:
        copy.start()
    lane = lax.broadcasted_iota(jnp.int32, (NEWT, HD), 1)
    tag = jnp.zeros((NEWT, HD), jnp.int32)
    for i in range(NEWT):
        tag = jnp.where(lane == line * NEWT + i, positions[i], tag)
    for side, digit in enumerate((tag // 32, tag % 32)):
        kv[side, HISTORY + NEWT :, :] = digit.astype(jnp.float32).astype(jnp.bfloat16)
    for copy in copies:
        copy.wait()


def spread_kernel(positions, kept, received, out):
    core, x_here = lax.axis_index("c"), lax.axis_index("x")
    row = lax.broadcasted_iota(jnp.int32, (8, HD), 0)
    tag = jnp.zeros((8, HD), jnp.int32)
    for i in range(TOKENS):
        position = positions[x_here * TOKENS + i]
        tag = jnp.where(row == 2 * i, position // 32, tag)
        tag = jnp.where(row == 2 * i + 1, position % 32, tag)
    tag = tag.astype(jnp.float32).astype(jnp.bfloat16)
    for x in range(XN):
        for other, array in ((0, kept), (1, received)):
            owner = core if other == 0 else 1 - core
            rows = array[:, x].reshape(OWN * GROUP, HD)
            first = pl.multiple_of(owner * OWN * GROUP, OWN * GROUP)
            for line in range(LINE):
                out[line * XN + x, pl.ds(first, OWN * GROUP), :] = rows
        for line in range(LINE):
            out[line * XN + x, BLOCK:, :] = tag


def join_kernel(own, lower, upper, three, two):
    for i, block in enumerate((own, lower, upper)):
        three[i] = block[...]
        if i < 2:
            two[i] = block[...]


def attend_kernel(page_slots, own, lower, upper, below, above, q, out, keys, values, scores):
    core, line = own_place()
    ctx = lax.axis_index("z") * YN + lax.axis_index("y")
    stride = jnp.where(core == 0, YN, 1)
    values[:, HD:] = jnp.ones((KEYS, HD), jnp.bfloat16)
    blocks = [own, lower, upper] + [below.at[i] for i in range(3)] + [above.at[i] for i in range(2)]
    high = jnp.zeros((NEWT, HD), jnp.float32)
    low = jnp.zeros((NEWT, HD), jnp.float32)
    count = jnp.int32(0)
    for block, offset in zip(blocks, OFFSETS, strict=True):
        source_line = lax.rem(line + offset + LINE, LINE)
        source = ctx + (source_line - line) * stride
        other = lax.rem(source + ZN * YN // 2, ZN * YN)
        first = pl.multiple_of(source_line * NEWT, NEWT)
        keys[pl.ds(first, NEWT), :] = block[0, HISTORY : HISTORY + NEWT, :]
        values[pl.ds(first, NEWT), :HD] = block[1, HISTORY : HISTORY + NEWT, :]
        high += block[0, HISTORY + NEWT :, :].astype(jnp.float32)
        low += block[1, HISTORY + NEWT :, :].astype(jnp.float32)
        candidates = [page_slots[2 * source], page_slots[2 * source + 1]]
        candidates += [page_slots[2 * other], page_slots[2 * other + 1]]
        for s in range(SLOTS):
            slot = source * SLOTS + s
            live = functools.reduce(jnp.logical_or, [candidate == slot for candidate in candidates])
            to = pl.multiple_of(FRESH + count * PAGE, PAGE)
            keys[pl.ds(to, PAGE), :] = block[0, s * PAGE : (s + 1) * PAGE, :]
            values[pl.ds(to, PAGE), :HD] = block[1, s * PAGE : (s + 1) * PAGE, :]
            count += live.astype(jnp.int32)
    key_at = (high * 32.0 + low)[0:1]
    places = functools.reduce(lambda size, less: jnp.where(count <= less, less, size), SIZES[-2::-1], SIZES[-1])

    def repeat(i, carry):
        here = pl.ds(pl.multiple_of(FRESH + i * PAGE, PAGE), PAGE)
        keys[here, :] = keys[FRESH : FRESH + PAGE, :]
        values[here, :] = jnp.zeros((PAGE, 2 * HD), jnp.bfloat16)
        return carry

    lax.fori_loop(count, places, repeat, 0)

    def chunks(pages):
        end = FRESH + pages * PAGE
        return [(start, min(CHUNK, end - start)) for start in range(0, end, CHUNK)]

    def score(part, side, pages):
        here = pl.ds(part * STEP_BLOCKS, STEP_BLOCKS)
        rows = q[here, :BLOCK, :].reshape(ROWS, HD)
        tags = q[here, BLOCK:, :].astype(jnp.float32)
        bias = []
        for t in range(TOKENS):
            query_at = tags[:, 2 * t, :] * 32.0 + tags[:, 2 * t + 1, :]
            hidden = jnp.where(key_at <= query_at, 0.0, LOWEST)
            bias.append(jnp.broadcast_to(hidden[:, None, :], (STEP_BLOCKS, GROUP, HD)))
        bias = jnp.stack(bias, axis=1).reshape(ROWS, HD)
        top = None
        for start, size in chunks(pages):
            product = lax.dot_general(
                rows, keys[start : start + size, :], (((1,), (1,)), ((), ())), preferred_element_type=jnp.float32
            )
            for j in range(0, size, HD):
                piece = product[:, j : j + HD]
                if start + j == 0:
                    piece = piece + bias
                scores[side, :, start + j : start + j + HD] = piece
                top = piece if top is None else jnp.maximum(top, piece)
        return top

    def weigh(part, side, pages, top):
        here = pl.ds(part * STEP_BLOCKS, STEP_BLOCKS)
        top = jnp.max(top, axis=1, keepdims=True) * TO_BITS
        summed = jnp.zeros((ROWS, 2 * HD), jnp.float32)
        for start, size in chunks(pages):
            weights = jnp.exp2(scores[side, :, start : start + size] * TO_BITS - top).astype(jnp.bfloat16)
            summed += jnp.dot(weights, values[start : start + size, :], preferred_element_type=jnp.float32)
        total = summed[:, HD:]
        out[here, :BLOCK, :] = (summed[:, :HD] / total).astype(jnp.bfloat16).reshape(STEP_BLOCKS, BLOCK, HD)
        level = (top + jnp.log2(total)).reshape(STEP_BLOCKS, BLOCK, HD)
        row = lax.broadcasted_iota(jnp.int32, (STEP_BLOCKS, BLOCK, HD), 1)
        lane = lax.broadcasted_iota(jnp.int32, (STEP_BLOCKS, BLOCK, HD), 2)
        level = jnp.sum(jnp.where(row == lane, level, 0.0), axis=1, keepdims=True)
        high = level.astype(jnp.bfloat16).astype(jnp.float32)
        rest = level - high
        middle = rest.astype(jnp.bfloat16).astype(jnp.float32)
        zeros = jnp.zeros((STEP_BLOCKS, 5, HD), jnp.float32)
        out[here, BLOCK:, :] = jnp.concatenate([high, middle, rest - middle, zeros], axis=1).astype(jnp.bfloat16)

    def attend_to(pages):
        def pair(i, carry):
            tops = [score(2 * i + side, side, pages) for side in range(2)]
            for side in range(2):
                weigh(2 * i + side, side, pages, tops[side])
            return carry

        lax.fori_loop(0, PARTS // 2, pair, 0)

    for pages in SIZES:
        pl.when(places == pages)(functools.partial(attend_to, pages))


def attend(page_slots, pieces, q):
    return call(
        attend_kernel,
        bf16(BLOCKS, WIRE, HD),
        megabytes=20,
        flops=2300000000,
        moved=5000000,
        in_specs=[SMEM] + [VMEM] * 6,
        scratch_shapes=[
            pltpu.VMEM((KEYS, HD), jnp.bfloat16),
            pltpu.VMEM((KEYS, 2 * HD), jnp.bfloat16),
            pltpu.VMEM((2, ROWS, KEYS), jnp.float32),
        ],
    )(page_slots, *pieces, q)


def combine_kernel(other, parts, out, merged_rows):
    owner = lax.axis_index("c") ^ other
    tags = parts[:, BLOCK:, :].astype(jnp.float32)
    level = tags[:, 0:1, :] + tags[:, 1:2, :] + tags[:, 2:3, :]
    level = level.reshape(LINE, XN, 1, HD)
    weight = jnp.exp2(level - jnp.max(level, axis=0, keepdims=True))
    weight = weight / jnp.sum(weight, axis=0, keepdims=True)
    row = lax.broadcasted_iota(jnp.int32, (BLOCK, HD), 0)
    lane = lax.broadcasted_iota(jnp.int32, (BLOCK, HD), 1)
    for x in range(XN):
        merged = jnp.zeros((BLOCK, HD), jnp.float32)
        for line in range(LINE):
            column = jnp.sum(jnp.where(row == lane, weight[line, x], 0.0), axis=1, keepdims=True)
            merged += column * parts[line * XN + x, :BLOCK, :].astype(jnp.float32)
        merged_rows[x] = merged.astype(jnp.bfloat16)
    for t in range(OWN):
        for x in range(XN):
            first = pl.multiple_of((owner * OWN + t) * GROUP, GROUP)
            out[t, x] = merged_rows[x, pl.ds(first, GROUP), :]


def finish_kernel(kept, received, out):
    core = lax.axis_index("c")
    for array, parity in ((kept, core), (received, 1 - core)):
        for t in range(OWN):
            for x in range(XN):
                first = pl.multiple_of((CN * x + parity) * GROUP, GROUP)
                out[t, pl.ds(first, GROUP), :] = array[t, x]


def body(queries, new_keys, new_values, new_positions, hist_keys, hist_values, page_slots):
    half = bf16(OWN, XN, GROUP, HD)
    sources = [
        queries.reshape(OWN, XN, CN, GROUP, HD),
        hist_keys.reshape(HISTORY, HD),
        hist_values.reshape(HISTORY, HD),
        new_keys.reshape(NEWT, HD),
        new_values.reshape(NEWT, HD),
    ]
    kv, q_kept, q_sent = call(
        pack_kernel,
        (bf16(2, KV_ROWS, HD), half, half),
        in_specs=[SMEM] + [HBM] * 5,
        scratch_shapes=[pltpu.SemaphoreType.DMA((6,))],
    )(new_positions, *(pltpu.with_memory_space_constraint(source, pltpu.HBM) for source in sources))
    lower = lax.ppermute(kv, ALL, along(3))
    upper = lax.ppermute(kv, ALL, along(-3))
    q_received = lax.ppermute(q_sent, ALL, SWAP)
    q = call(spread_kernel, bf16(BLOCKS, WIRE, HD), in_specs=[SMEM, VMEM, VMEM])(
        new_positions, q_kept, q_received
    )
    three, two = call(join_kernel, (bf16(3, 2, KV_ROWS, HD), bf16(2, 2, KV_ROWS, HD)), flops=30000000000)(kv, lower, upper)
    q = lax.all_to_all(q, ALL, split_axis=0, concat_axis=0, axis_index_groups=CROSS, tiled=True)
    below = lax.ppermute(three, ALL, along(1))
    above = lax.ppermute(two, ALL, along(-1))
    parts = attend(page_slots, (kv, lower, upper, below, above), q)
    parts = lax.all_to_all(parts, ALL, split_axis=0, concat_axis=0, axis_index_groups=CROSS, tiled=True)

    def combined(other):
        return call(
            functools.partial(combine_kernel, other),
            half,
            scratch_shapes=[pltpu.VMEM((XN, BLOCK, HD), jnp.bfloat16)],
        )(parts)

    received = lax.ppermute(combined(1), ALL, SWAP)
    return call(finish_kernel, bf16(OWN, HEADS, HD))(combined(0), received)


def solution(mesh):
    split = Mesh(mesh.devices.reshape(ZN, YN, XN, CN), ALL)
    ctx, kvh = ("z", "y"), ("x", "c")
    in_specs = (
        P(ctx + kvh, None, None),
        P(ctx, kvh, None),
        P(ctx, kvh, None),
        P(ctx),
        P(ctx, None, kvh, None),
        P(ctx, None, kvh, None),
        P(),
    )
    return jax.shard_map(body, mesh=split, in_specs=in_specs, out_specs=P(ctx + kvh, None, None), check_vma=False)
```

```python
import functools
import math

import jax
import jax.numpy as jnp
import numpy as np
from jax import lax
from jax.experimental import pallas as pl
from jax.experimental.pallas import tpu as pltpu
from jax.sharding import Mesh, PartitionSpec as P

ZN, YN, XN, CN = 8, 8, 4, 2
LINE = 8
KN = XN * CN
ALL = ("z", "y", "x", "c")
HEADS, GROUP, HD, PAGE, SLOTS, NEWT = 128, 16, 128, 128, 3, 16
HISTORY = SLOTS * PAGE
KV_ROWS = HISTORY + 2 * NEWT
FRESH = LINE * NEWT
MOST_PAGES = LINE * SLOTS
KEYS = FRESH + MOST_PAGES * PAGE
OWN = 2
TOKENS = OWN * CN
BLOCK = TOKENS * GROUP
LINE_ROWS = NEWT * GROUP
LINE_WIRE = LINE_ROWS + 2 * NEWT
WIRE = BLOCK + 8
BLOCKS = LINE * XN
STEP_LINES = 2
STEP_BLOCKS = STEP_LINES * XN
ROWS = STEP_BLOCKS * BLOCK
PARTS = BLOCKS // STEP_BLOCKS
CHUNK = 512
SIZES = (16, 18, 20, 24)
OFFSETS = (0, -3, 2, 1, -2, 3, -1, -4)
TO_BITS = math.log2(math.e) / math.sqrt(HD)
LOWEST = -1e30
JOIN = 30000000000

IDS = np.arange(ZN * YN * XN * CN).reshape(ZN, YN, XN, CN)
CROSS = [IDS[z, :, :, 0].ravel().tolist() for z in range(ZN)] + [IDS[:, y, :, 1].ravel().tolist() for y in range(YN)]

CROSS_LINES = [IDS[z, :, x, 0].tolist() for z in range(ZN) for x in range(XN)]
CROSS_LINES += [IDS[:, y, x, 1].tolist() for y in range(YN) for x in range(XN)]


def along(distance):
    route = []
    for z in range(ZN):
        for y in range(YN):
            for x in range(XN):
                route.append((int(IDS[z, y, x, 0]), int(IDS[(z + distance) % ZN, y, x, 0])))
                route.append((int(IDS[z, y, x, 1]), int(IDS[z, (y + distance) % YN, x, 1])))
    return route


SWAP = [(int(i), int(i) ^ 1) for i in IDS.ravel()]


def call(kernel, out_shape, megabytes=16, flops=1000000, moved=800000, **options):
    return pl.pallas_call(
        kernel,
        out_shape=out_shape,
        compiler_params=pltpu.CompilerParams(vmem_limit_bytes=megabytes * 1024 * 1024),
        cost_estimate=pl.CostEstimate(flops=flops, bytes_accessed=moved, transcendentals=flops // 500),
        **options,
    )


def bf16(*shape):
    return jax.ShapeDtypeStruct(shape, jnp.bfloat16)


SMEM = pl.BlockSpec(memory_space=pltpu.SMEM)
HBM = pl.BlockSpec(memory_space=pltpu.HBM)
VMEM = pl.BlockSpec(memory_space=pltpu.VMEM)


def own_place():
    core = lax.axis_index("c")
    return core, jnp.where(core == 0, lax.axis_index("z"), lax.axis_index("y"))


def pack_kernel(positions, queries, hist_keys, hist_values, new_keys, new_values, kv, sent, tags, at, arrived):
    core, line = own_place()
    first = pltpu.make_async_copy(positions, at, arrived.at[6])
    copies = [
        pltpu.make_async_copy(hist_keys, kv.at[0, pl.ds(0, HISTORY)], arrived.at[0]),
        pltpu.make_async_copy(hist_values, kv.at[1, pl.ds(0, HISTORY)], arrived.at[1]),
        pltpu.make_async_copy(new_keys, kv.at[0, pl.ds(HISTORY, NEWT)], arrived.at[2]),
        pltpu.make_async_copy(new_values, kv.at[1, pl.ds(HISTORY, NEWT)], arrived.at[3]),
        pltpu.make_async_copy(queries.at[0], sent.at[:, 0], arrived.at[4]),
        pltpu.make_async_copy(queries.at[1], sent.at[:, 1], arrived.at[5]),
    ]
    for copy in [first] + copies:
        copy.start()
    first.wait()
    lane = lax.broadcasted_iota(jnp.int32, (NEWT, HD), 1)
    row = lax.broadcasted_iota(jnp.int32, (NEWT, HD), 0)
    key_tag = jnp.zeros((NEWT, HD), jnp.int32)
    query_tag = jnp.zeros((NEWT, HD), jnp.int32)
    for i in range(NEWT):
        key_tag = jnp.where(lane == line * NEWT + i, at[i], key_tag)
        query_tag = jnp.where(row == i, at[i], query_tag)
    for side, digit in enumerate((lambda tag: tag // 32, lambda tag: tag % 32)):
        kv[side, HISTORY + NEWT :, :] = digit(key_tag).astype(jnp.float32).astype(jnp.bfloat16)
        tags[side * NEWT : (side + 1) * NEWT, :] = digit(query_tag).astype(jnp.float32).astype(jnp.bfloat16)
    for copy in copies:
        copy.wait()


def spread_kernel(queries, tags, out, done):
    copies = []
    for line in range(LINE):
        copies.append(pltpu.make_async_copy(queries, out.at[line, pl.ds(0, LINE_ROWS)], done.at[2 * line]))
        copies.append(pltpu.make_async_copy(tags, out.at[line, pl.ds(LINE_ROWS, 2 * NEWT)], done.at[2 * line + 1]))
    for copy in copies:
        copy.start()
    for copy in copies:
        copy.wait()


def join_kernel(own, lower, upper, three, two):
    for i, block in enumerate((own, lower, upper)):
        three[i] = block[...]
        if i < 2:
            two[i] = block[...]


def attend_kernel(page_slots, own, lower, upper, above, below, q, out, keys, values, scores):
    core, line = own_place()
    ctx = lax.axis_index("z") * YN + lax.axis_index("y")
    stride = jnp.where(core == 0, YN, 1)
    values[:, HD:] = jnp.ones((KEYS, HD), jnp.bfloat16)
    blocks = [own, lower, upper] + [above.at[i] for i in range(3)] + [below.at[i] for i in range(2)]
    high = jnp.zeros((NEWT, HD), jnp.float32)
    low = jnp.zeros((NEWT, HD), jnp.float32)
    count = jnp.int32(0)
    for block, offset in zip(blocks, OFFSETS, strict=True):
        source_line = lax.rem(line + offset + LINE, LINE)
        source = ctx + (source_line - line) * stride
        other = lax.rem(source + ZN * YN // 2, ZN * YN)
        first = pl.multiple_of(source_line * NEWT, NEWT)
        keys[pl.ds(first, NEWT), :] = block[0, HISTORY : HISTORY + NEWT, :]
        values[pl.ds(first, NEWT), :HD] = block[1, HISTORY : HISTORY + NEWT, :]
        high += block[0, HISTORY + NEWT :, :].astype(jnp.float32)
        low += block[1, HISTORY + NEWT :, :].astype(jnp.float32)
        candidates = [page_slots[2 * source], page_slots[2 * source + 1]]
        candidates += [page_slots[2 * other], page_slots[2 * other + 1]]
        for s in range(SLOTS):
            slot = source * SLOTS + s
            live = functools.reduce(jnp.logical_or, [candidate == slot for candidate in candidates])
            to = pl.multiple_of(FRESH + count * PAGE, PAGE)
            keys[pl.ds(to, PAGE), :] = block[0, s * PAGE : (s + 1) * PAGE, :]
            values[pl.ds(to, PAGE), :HD] = block[1, s * PAGE : (s + 1) * PAGE, :]
            count += live.astype(jnp.int32)
    key_at = (high * 32.0 + low)[0:1]
    places = functools.reduce(lambda size, less: jnp.where(count <= less, less, size), SIZES[-2::-1], SIZES[-1])

    def repeat(i, carry):
        here = pl.ds(pl.multiple_of(FRESH + i * PAGE, PAGE), PAGE)
        keys[here, :] = keys[FRESH : FRESH + PAGE, :]
        values[here, :] = jnp.zeros((PAGE, 2 * HD), jnp.bfloat16)
        return carry

    lax.fori_loop(count, places, repeat, 0)

    def chunks(pages):
        end = FRESH + pages * PAGE
        return [(start, min(CHUNK, end - start)) for start in range(0, end, CHUNK)]

    def score(part, side, pages):
        here = pl.ds(part * STEP_LINES, STEP_LINES)
        rows = q[here, :LINE_ROWS, :].reshape(ROWS, HD)
        tags = q[here, LINE_ROWS:, :].astype(jnp.float32)
        query_at = tags[:, :NEWT, :] * 32.0 + tags[:, NEWT:, :]
        hidden = jnp.where(key_at <= query_at, 0.0, LOWEST)
        bias = jnp.broadcast_to(hidden[:, :, None, :], (STEP_LINES, NEWT, GROUP, HD)).reshape(ROWS, HD)
        top = None
        for start, size in chunks(pages):
            product = lax.dot_general(
                rows, keys[start : start + size, :], (((1,), (1,)), ((), ())), preferred_element_type=jnp.float32
            )
            for j in range(0, size, HD):
                piece = product[:, j : j + HD]
                if start + j == 0:
                    piece = piece + bias
                scores[side, :, start + j : start + j + HD] = piece
                top = piece if top is None else jnp.maximum(top, piece)
        return top

    def weigh(part, side, pages, top):
        here = pl.ds(part * STEP_BLOCKS, STEP_BLOCKS)
        top = jnp.max(top, axis=1, keepdims=True) * TO_BITS
        summed = jnp.zeros((ROWS, 2 * HD), jnp.float32)
        for start, size in chunks(pages):
            weights = jnp.exp2(scores[side, :, start : start + size] * TO_BITS - top).astype(jnp.bfloat16)
            summed += jnp.dot(weights, values[start : start + size, :], preferred_element_type=jnp.float32)
        total = summed[:, HD:]
        out[here, :BLOCK, :] = (summed[:, :HD] / total).astype(jnp.bfloat16).reshape(STEP_BLOCKS, BLOCK, HD)
        level = (top + jnp.log2(total)).reshape(STEP_BLOCKS, BLOCK, HD)
        row = lax.broadcasted_iota(jnp.int32, (STEP_BLOCKS, BLOCK, HD), 1)
        lane = lax.broadcasted_iota(jnp.int32, (STEP_BLOCKS, BLOCK, HD), 2)
        level = jnp.sum(jnp.where(row == lane, level, 0.0), axis=1, keepdims=True)
        high = level.astype(jnp.bfloat16).astype(jnp.float32)
        rest = level - high
        middle = rest.astype(jnp.bfloat16).astype(jnp.float32)
        zeros = jnp.zeros((STEP_BLOCKS, 5, HD), jnp.float32)
        out[here, BLOCK:, :] = jnp.concatenate([high, middle, rest - middle, zeros], axis=1).astype(jnp.bfloat16)

    def attend_to(pages):
        def pair(i, carry):
            tops = [score(2 * i + side, side, pages) for side in range(2)]
            for side in range(2):
                weigh(2 * i + side, side, pages, tops[side])
            return carry

        lax.fori_loop(0, PARTS // 2, pair, 0)

    for pages in SIZES:
        pl.when(places == pages)(functools.partial(attend_to, pages))


def attend(page_slots, pieces, q):
    return call(
        attend_kernel,
        bf16(BLOCKS, WIRE, HD),
        megabytes=20,
        flops=2300000000,
        moved=5000000,
        in_specs=[SMEM] + [VMEM] * 6,
        scratch_shapes=[
            pltpu.VMEM((KEYS, HD), jnp.bfloat16),
            pltpu.VMEM((KEYS, 2 * HD), jnp.bfloat16),
            pltpu.VMEM((2, ROWS, KEYS), jnp.float32),
        ],
    )(page_slots, *pieces, q)


def combine_kernel(other, parts, out, merged_rows):
    owner = lax.axis_index("c") ^ other
    tags = parts[:, BLOCK:, :].astype(jnp.float32)
    level = tags[:, 0:1, :] + tags[:, 1:2, :] + tags[:, 2:3, :]
    level = level.reshape(LINE, XN, 1, HD)
    weight = jnp.exp2(level - jnp.max(level, axis=0, keepdims=True))
    weight = weight / jnp.sum(weight, axis=0, keepdims=True)
    row = lax.broadcasted_iota(jnp.int32, (BLOCK, HD), 0)
    lane = lax.broadcasted_iota(jnp.int32, (BLOCK, HD), 1)
    for x in range(XN):
        merged = jnp.zeros((BLOCK, HD), jnp.float32)
        for line in range(LINE):
            column = jnp.sum(jnp.where(row == lane, weight[line, x], 0.0), axis=1, keepdims=True)
            merged += column * parts[line * XN + x, :BLOCK, :].astype(jnp.float32)
        merged_rows[x] = merged.astype(jnp.bfloat16)
    for t in range(OWN):
        for x in range(XN):
            first = pl.multiple_of((owner * OWN + t) * GROUP, GROUP)
            out[t, x] = merged_rows[x, pl.ds(first, GROUP), :]


def finish_kernel(kept, received, out):
    core = lax.axis_index("c")
    for array, parity in ((kept, core), (received, 1 - core)):
        for t in range(OWN):
            for x in range(XN):
                first = pl.multiple_of((CN * x + parity) * GROUP, GROUP)
                out[t, pl.ds(first, GROUP), :] = array[t, x]


def body(queries, new_keys, new_values, new_positions, hist_keys, hist_values, page_slots):
    half = bf16(OWN, XN, GROUP, HD)
    sources = [
        new_positions,
        queries.reshape(OWN, KN, GROUP, HD),
        hist_keys.reshape(HISTORY, HD),
        hist_values.reshape(HISTORY, HD),
        new_keys.reshape(NEWT, HD),
        new_values.reshape(NEWT, HD),
    ]
    kv, q_sent, tags = call(
        pack_kernel,
        (bf16(2, KV_ROWS, HD), bf16(KN, OWN, GROUP, HD), bf16(2 * NEWT, HD)),
        in_specs=[HBM] * 6,
        scratch_shapes=[pltpu.SMEM((NEWT,), jnp.int32), pltpu.SemaphoreType.DMA((7,))],
    )(*(pltpu.with_memory_space_constraint(source, pltpu.HBM) for source in sources))
    lower = lax.ppermute(kv, ALL, along(3))
    upper = lax.ppermute(kv, ALL, along(-2))
    q = lax.all_to_all(q_sent, ("x", "c"), split_axis=0, concat_axis=0, tiled=True)
    q = call(
        spread_kernel,
        bf16(LINE, LINE_WIRE, HD),
        out_specs=HBM,
        scratch_shapes=[pltpu.SemaphoreType.DMA((2 * LINE,))],
    )(q.reshape(LINE_ROWS, HD), tags)
    q = lax.all_to_all(q, ALL, split_axis=0, concat_axis=0, axis_index_groups=CROSS_LINES, tiled=True)
    three, two = call(join_kernel, (bf16(3, 2, KV_ROWS, HD), bf16(2, 2, KV_ROWS, HD)), flops=JOIN)(kv, lower, upper)
    above = lax.ppermute(three, ALL, along(-1))
    below = lax.ppermute(two, ALL, along(1))
    parts = attend(page_slots, (kv, lower, upper, above, below), q)
    parts = lax.all_to_all(parts, ALL, split_axis=0, concat_axis=0, axis_index_groups=CROSS, tiled=True)

    def combined(other):
        return call(
            functools.partial(combine_kernel, other),
            half,
            scratch_shapes=[pltpu.VMEM((XN, BLOCK, HD), jnp.bfloat16)],
        )(parts)

    received = lax.ppermute(combined(1), ALL, SWAP)
    return call(finish_kernel, bf16(OWN, HEADS, HD))(combined(0), received)


def solution(mesh):
    split = Mesh(mesh.devices.reshape(ZN, YN, XN, CN), ALL)
    ctx, kvh = ("z", "y"), ("x", "c")
    in_specs = (
        P(ctx + kvh, None, None),
        P(ctx, kvh, None),
        P(ctx, kvh, None),
        P(ctx),
        P(ctx, None, kvh, None),
        P(ctx, None, kvh, None),
        P(),
    )
    return jax.shard_map(body, mesh=split, in_specs=in_specs, out_specs=P(ctx + kvh, None, None), check_vma=False)
```

```python
import functools
import math

import jax
import jax.numpy as jnp
import numpy as np
from jax import lax
from jax.experimental import pallas as pl
from jax.experimental.pallas import tpu as pltpu
from jax.sharding import Mesh, PartitionSpec as P

ZN, YN, XN, CN = 8, 8, 4, 2
LINE = 8
ALL = ("z", "y", "x", "c")
HEADS, GROUP, HD, PAGE, SLOTS, NEWT = 128, 16, 128, 128, 3, 16
HISTORY = SLOTS * PAGE
KV_ROWS = HISTORY + 2 * NEWT
FRESH = LINE * NEWT
MOST_PAGES = LINE * SLOTS
KEYS = FRESH + MOST_PAGES * PAGE
OWN = 2
TOKENS = OWN * CN
BLOCK = TOKENS * GROUP
WIRE = BLOCK + 8
BLOCKS = LINE * XN
STEP_BLOCKS = 8
ROWS = STEP_BLOCKS * BLOCK
PARTS = BLOCKS // STEP_BLOCKS
CHUNK = 512
SIZES = (16, 18, 20, 24)
OFFSETS = (0, -3, 2, 1, -2, 3, -1, -4)
TO_BITS = math.log2(math.e) / math.sqrt(HD)
LOWEST = -1e30
JOIN = 30000000000

IDS = np.arange(ZN * YN * XN * CN).reshape(ZN, YN, XN, CN)
CROSS = [IDS[z, :, :, 0].ravel().tolist() for z in range(ZN)] + [IDS[:, y, :, 1].ravel().tolist() for y in range(YN)]


def along(distance):
    route = []
    for z in range(ZN):
        for y in range(YN):
            for x in range(XN):
                route.append((int(IDS[z, y, x, 0]), int(IDS[(z + distance) % ZN, y, x, 0])))
                route.append((int(IDS[z, y, x, 1]), int(IDS[z, (y + distance) % YN, x, 1])))
    return route


SWAP = [(int(i), int(i) ^ 1) for i in IDS.ravel()]


def call(kernel, out_shape, megabytes=16, flops=1000000, moved=800000, **options):
    return pl.pallas_call(
        kernel,
        out_shape=out_shape,
        compiler_params=pltpu.CompilerParams(vmem_limit_bytes=megabytes * 1024 * 1024),
        cost_estimate=pl.CostEstimate(flops=flops, bytes_accessed=moved, transcendentals=flops // 500),
        **options,
    )


def bf16(*shape):
    return jax.ShapeDtypeStruct(shape, jnp.bfloat16)


SMEM = pl.BlockSpec(memory_space=pltpu.SMEM)
HBM = pl.BlockSpec(memory_space=pltpu.HBM)
VMEM = pl.BlockSpec(memory_space=pltpu.VMEM)


def own_place():
    core = lax.axis_index("c")
    return core, jnp.where(core == 0, lax.axis_index("z"), lax.axis_index("y"))


def pack_kernel(
    positions, queries, hist_keys, hist_values, new_keys, new_values, kv, kept, sent, tags, at, arrived
):
    core, line = own_place()
    first = pltpu.make_async_copy(positions, at, arrived.at[6])
    copies = [
        pltpu.make_async_copy(hist_keys, kv.at[0, pl.ds(0, HISTORY)], arrived.at[0]),
        pltpu.make_async_copy(hist_values, kv.at[1, pl.ds(0, HISTORY)], arrived.at[1]),
        pltpu.make_async_copy(new_keys, kv.at[0, pl.ds(HISTORY, NEWT)], arrived.at[2]),
        pltpu.make_async_copy(new_values, kv.at[1, pl.ds(HISTORY, NEWT)], arrived.at[3]),
        pltpu.make_async_copy(queries.at[:, :, core], kept, arrived.at[4]),
        pltpu.make_async_copy(queries.at[:, :, 1 - core], sent, arrived.at[5]),
    ]
    for copy in [first] + copies:
        copy.start()
    first.wait()
    lane = lax.broadcasted_iota(jnp.int32, (NEWT, HD), 1)
    row = lax.broadcasted_iota(jnp.int32, (8, HD), 0)
    key_tag = jnp.zeros((NEWT, HD), jnp.int32)
    for i in range(NEWT):
        key_tag = jnp.where(lane == line * NEWT + i, at[i], key_tag)
    for side, digit in enumerate((key_tag // 32, key_tag % 32)):
        kv[side, HISTORY + NEWT :, :] = digit.astype(jnp.float32).astype(jnp.bfloat16)
    query_tag = jnp.zeros((8, HD), jnp.int32)
    for i in range(TOKENS):
        position = at[lax.axis_index("x") * TOKENS + i]
        query_tag = jnp.where(row == i, position // 32, query_tag)
        query_tag = jnp.where(row == TOKENS + i, position % 32, query_tag)
    tags[...] = query_tag.astype(jnp.float32).astype(jnp.bfloat16)
    for copy in copies:
        copy.wait()


def spread_kernel(kept, received, tags, out, blocks, done):
    core = lax.axis_index("c")
    for x in range(XN):
        for owner, array in ((core, kept), (1 - core, received)):
            first = pl.multiple_of(owner * OWN * GROUP, OWN * GROUP)
            blocks[x, pl.ds(first, OWN * GROUP), :] = array[:, x].reshape(OWN * GROUP, HD)
        blocks[x, BLOCK:, :] = tags[...]
    copies = [
        pltpu.make_async_copy(blocks, out.at[pl.ds(line * XN, XN)], done.at[line]) for line in range(LINE)
    ]
    for copy in copies:
        copy.start()
    for copy in copies:
        copy.wait()


def join_kernel(own, lower, upper, three, two):
    for i, block in enumerate((own, lower, upper)):
        three[i] = block[...]
        if i < 2:
            two[i] = block[...]


def attend_kernel(page_slots, own, lower, upper, above, below, q, out, keys, values, scores):
    core, line = own_place()
    ctx = lax.axis_index("z") * YN + lax.axis_index("y")
    stride = jnp.where(core == 0, YN, 1)
    values[:, HD:] = jnp.ones((KEYS, HD), jnp.bfloat16)
    blocks = [own, lower, upper] + [above.at[i] for i in range(3)] + [below.at[i] for i in range(2)]
    high = jnp.zeros((NEWT, HD), jnp.float32)
    low = jnp.zeros((NEWT, HD), jnp.float32)
    count = jnp.int32(0)
    for block, offset in zip(blocks, OFFSETS, strict=True):
        source_line = lax.rem(line + offset + LINE, LINE)
        source = ctx + (source_line - line) * stride
        other = lax.rem(source + ZN * YN // 2, ZN * YN)
        first = pl.multiple_of(source_line * NEWT, NEWT)
        keys[pl.ds(first, NEWT), :] = block[0, HISTORY : HISTORY + NEWT, :]
        values[pl.ds(first, NEWT), :HD] = block[1, HISTORY : HISTORY + NEWT, :]
        high += block[0, HISTORY + NEWT :, :].astype(jnp.float32)
        low += block[1, HISTORY + NEWT :, :].astype(jnp.float32)
        candidates = [page_slots[2 * source], page_slots[2 * source + 1]]
        candidates += [page_slots[2 * other], page_slots[2 * other + 1]]
        for s in range(SLOTS):
            slot = source * SLOTS + s
            live = functools.reduce(jnp.logical_or, [candidate == slot for candidate in candidates])
            to = pl.multiple_of(FRESH + count * PAGE, PAGE)
            keys[pl.ds(to, PAGE), :] = block[0, s * PAGE : (s + 1) * PAGE, :]
            values[pl.ds(to, PAGE), :HD] = block[1, s * PAGE : (s + 1) * PAGE, :]
            count += live.astype(jnp.int32)
    key_at = (high * 32.0 + low)[0:1]
    places = functools.reduce(lambda size, less: jnp.where(count <= less, less, size), SIZES[-2::-1], SIZES[-1])

    def repeat(i, carry):
        here = pl.ds(pl.multiple_of(FRESH + i * PAGE, PAGE), PAGE)
        keys[here, :] = keys[FRESH : FRESH + PAGE, :]
        values[here, :] = jnp.zeros((PAGE, 2 * HD), jnp.bfloat16)
        return carry

    lax.fori_loop(count, places, repeat, 0)

    def chunks(pages):
        end = FRESH + pages * PAGE
        return [(start, min(CHUNK, end - start)) for start in range(0, end, CHUNK)]

    def score(part, side, pages):
        here = pl.ds(part * STEP_BLOCKS, STEP_BLOCKS)
        rows = q[here, :BLOCK, :].reshape(ROWS, HD)
        tags = q[here, BLOCK:, :].astype(jnp.float32)
        query_at = tags[:, :TOKENS, :] * 32.0 + tags[:, TOKENS:, :]
        hidden = jnp.where(key_at <= query_at, 0.0, LOWEST)
        bias = jnp.broadcast_to(hidden[:, :, None, :], (STEP_BLOCKS, TOKENS, GROUP, HD)).reshape(ROWS, HD)
        top = None
        for start, size in chunks(pages):
            product = lax.dot_general(
                rows, keys[start : start + size, :], (((1,), (1,)), ((), ())), preferred_element_type=jnp.float32
            )
            for j in range(0, size, HD):
                piece = product[:, j : j + HD]
                if start + j == 0:
                    piece = piece + bias
                scores[side, :, start + j : start + j + HD] = piece
                top = piece if top is None else jnp.maximum(top, piece)
        return top

    def weigh(part, side, pages, top):
        here = pl.ds(part * STEP_BLOCKS, STEP_BLOCKS)
        top = jnp.max(top, axis=1, keepdims=True) * TO_BITS
        summed = jnp.zeros((ROWS, 2 * HD), jnp.float32)
        for start, size in chunks(pages):
            weights = jnp.exp2(scores[side, :, start : start + size] * TO_BITS - top).astype(jnp.bfloat16)
            summed += jnp.dot(weights, values[start : start + size, :], preferred_element_type=jnp.float32)
        total = summed[:, HD:]
        out[here, :BLOCK, :] = (summed[:, :HD] / total).astype(jnp.bfloat16).reshape(STEP_BLOCKS, BLOCK, HD)
        level = (top + jnp.log2(total)).reshape(STEP_BLOCKS, BLOCK, HD)
        row = lax.broadcasted_iota(jnp.int32, (STEP_BLOCKS, BLOCK, HD), 1)
        lane = lax.broadcasted_iota(jnp.int32, (STEP_BLOCKS, BLOCK, HD), 2)
        level = jnp.sum(jnp.where(row == lane, level, 0.0), axis=1, keepdims=True)
        high = level.astype(jnp.bfloat16).astype(jnp.float32)
        rest = level - high
        middle = rest.astype(jnp.bfloat16).astype(jnp.float32)
        zeros = jnp.zeros((STEP_BLOCKS, 5, HD), jnp.float32)
        out[here, BLOCK:, :] = jnp.concatenate([high, middle, rest - middle, zeros], axis=1).astype(jnp.bfloat16)

    def attend_to(pages):
        def pair(i, carry):
            tops = [score(2 * i + side, side, pages) for side in range(2)]
            for side in range(2):
                weigh(2 * i + side, side, pages, tops[side])
            return carry

        lax.fori_loop(0, PARTS // 2, pair, 0)

    for pages in SIZES:
        pl.when(places == pages)(functools.partial(attend_to, pages))


def attend(page_slots, pieces, q):
    return call(
        attend_kernel,
        bf16(BLOCKS, WIRE, HD),
        megabytes=20,
        flops=2300000000,
        moved=5000000,
        in_specs=[SMEM] + [VMEM] * 6,
        scratch_shapes=[
            pltpu.VMEM((KEYS, HD), jnp.bfloat16),
            pltpu.VMEM((KEYS, 2 * HD), jnp.bfloat16),
            pltpu.VMEM((2, ROWS, KEYS), jnp.float32),
        ],
    )(page_slots, *pieces, q)


def combine_kernel(other, parts, out, merged_rows):
    owner = lax.axis_index("c") ^ other
    tags = parts[:, BLOCK:, :].astype(jnp.float32)
    level = tags[:, 0:1, :] + tags[:, 1:2, :] + tags[:, 2:3, :]
    level = level.reshape(LINE, XN, 1, HD)
    weight = jnp.exp2(level - jnp.max(level, axis=0, keepdims=True))
    weight = weight / jnp.sum(weight, axis=0, keepdims=True)
    row = lax.broadcasted_iota(jnp.int32, (BLOCK, HD), 0)
    lane = lax.broadcasted_iota(jnp.int32, (BLOCK, HD), 1)
    for x in range(XN):
        merged = jnp.zeros((BLOCK, HD), jnp.float32)
        for line in range(LINE):
            column = jnp.sum(jnp.where(row == lane, weight[line, x], 0.0), axis=1, keepdims=True)
            merged += column * parts[line * XN + x, :BLOCK, :].astype(jnp.float32)
        merged_rows[x] = merged.astype(jnp.bfloat16)
    for t in range(OWN):
        for x in range(XN):
            first = pl.multiple_of((owner * OWN + t) * GROUP, GROUP)
            out[t, x] = merged_rows[x, pl.ds(first, GROUP), :]


def finish_kernel(kept, received, out):
    core = lax.axis_index("c")
    for array, parity in ((kept, core), (received, 1 - core)):
        for t in range(OWN):
            for x in range(XN):
                first = pl.multiple_of((CN * x + parity) * GROUP, GROUP)
                out[t, pl.ds(first, GROUP), :] = array[t, x]


def body(queries, new_keys, new_values, new_positions, hist_keys, hist_values, page_slots):
    half = bf16(OWN, XN, GROUP, HD)
    sources = [
        new_positions,
        queries.reshape(OWN, XN, CN, GROUP, HD),
        hist_keys.reshape(HISTORY, HD),
        hist_values.reshape(HISTORY, HD),
        new_keys.reshape(NEWT, HD),
        new_values.reshape(NEWT, HD),
    ]
    kv, q_kept, q_sent, tags = call(
        pack_kernel,
        (bf16(2, KV_ROWS, HD), half, half, bf16(8, HD)),
        in_specs=[HBM] * 6,
        scratch_shapes=[pltpu.SMEM((NEWT,), jnp.int32), pltpu.SemaphoreType.DMA((7,))],
    )(*(pltpu.with_memory_space_constraint(source, pltpu.HBM) for source in sources))
    lower = lax.ppermute(kv, ALL, along(3))
    upper = lax.ppermute(kv, ALL, along(-2))
    q_received = lax.ppermute(q_sent, ALL, SWAP)
    q = call(
        spread_kernel,
        bf16(BLOCKS, WIRE, HD),
        out_specs=HBM,
        scratch_shapes=[pltpu.VMEM((XN, WIRE, HD), jnp.bfloat16), pltpu.SemaphoreType.DMA((LINE,))],
    )(q_kept, q_received, tags)
    q = lax.all_to_all(q, ALL, split_axis=0, concat_axis=0, axis_index_groups=CROSS, tiled=True)
    three, two = call(join_kernel, (bf16(3, 2, KV_ROWS, HD), bf16(2, 2, KV_ROWS, HD)), flops=JOIN)(kv, lower, upper)
    above = lax.ppermute(three, ALL, along(-1))
    below = lax.ppermute(two, ALL, along(1))
    parts = attend(page_slots, (kv, lower, upper, above, below), q)
    parts = lax.all_to_all(parts, ALL, split_axis=0, concat_axis=0, axis_index_groups=CROSS, tiled=True)

    def combined(other):
        return call(
            functools.partial(combine_kernel, other),
            half,
            scratch_shapes=[pltpu.VMEM((XN, BLOCK, HD), jnp.bfloat16)],
        )(parts)

    received = lax.ppermute(combined(1), ALL, SWAP)
    return call(finish_kernel, bf16(OWN, HEADS, HD))(combined(0), received)


def solution(mesh):
    split = Mesh(mesh.devices.reshape(ZN, YN, XN, CN), ALL)
    ctx, kvh = ("z", "y"), ("x", "c")
    in_specs = (
        P(ctx + kvh, None, None),
        P(ctx, kvh, None),
        P(ctx, kvh, None),
        P(ctx),
        P(ctx, None, kvh, None),
        P(ctx, None, kvh, None),
        P(),
    )
    return jax.shard_map(body, mesh=split, in_specs=in_specs, out_specs=P(ctx + kvh, None, None), check_vma=False)
```

```python
import functools
import math

import jax
import jax.numpy as jnp
import numpy as np
from jax import lax
from jax.experimental import pallas as pl
from jax.experimental.pallas import tpu as pltpu
from jax.sharding import Mesh, PartitionSpec as P

ZN, YN, XN, CN = 8, 8, 4, 2
LINE = 8
ALL = ("z", "y", "x", "c")
HEADS, GROUP, HD, PAGE, SLOTS, NEWT = 128, 16, 128, 128, 3, 16
HISTORY = SLOTS * PAGE
KV_ROWS = HISTORY + 2 * NEWT
FRESH = LINE * NEWT
MOST_PAGES = LINE * SLOTS
KEYS = FRESH + MOST_PAGES * PAGE
OWN = 2
TOKENS = OWN * CN
BLOCK = TOKENS * GROUP
WIRE = BLOCK + 8
BLOCKS = LINE * XN
STEP_BLOCKS = 8
ROWS = STEP_BLOCKS * BLOCK
PARTS = BLOCKS // STEP_BLOCKS
CHUNK = 512
SIZES = (16, 18, 20, 24)
OFFSETS = (0, -3, 2, 1, -2, 3, -1, -4)
TO_BITS = math.log2(math.e) / math.sqrt(HD)
LOWEST = -1e30
JOIN = 30000000000

IDS = np.arange(ZN * YN * XN * CN).reshape(ZN, YN, XN, CN)
CROSS = [IDS[z, :, :, 0].ravel().tolist() for z in range(ZN)] + [IDS[:, y, :, 1].ravel().tolist() for y in range(YN)]


def along(distance):
    route = []
    for z in range(ZN):
        for y in range(YN):
            for x in range(XN):
                route.append((int(IDS[z, y, x, 0]), int(IDS[(z + distance) % ZN, y, x, 0])))
                route.append((int(IDS[z, y, x, 1]), int(IDS[z, (y + distance) % YN, x, 1])))
    return route


SWAP = [(int(i), int(i) ^ 1) for i in IDS.ravel()]


def call(kernel, out_shape, megabytes=16, flops=1000000, moved=800000, **options):
    return pl.pallas_call(
        kernel,
        out_shape=out_shape,
        compiler_params=pltpu.CompilerParams(vmem_limit_bytes=megabytes * 1024 * 1024),
        cost_estimate=pl.CostEstimate(flops=flops, bytes_accessed=moved, transcendentals=flops // 500),
        **options,
    )


def bf16(*shape):
    return jax.ShapeDtypeStruct(shape, jnp.bfloat16)


SMEM = pl.BlockSpec(memory_space=pltpu.SMEM)
HBM = pl.BlockSpec(memory_space=pltpu.HBM)
VMEM = pl.BlockSpec(memory_space=pltpu.VMEM)


def own_place():
    core = lax.axis_index("c")
    return core, jnp.where(core == 0, lax.axis_index("z"), lax.axis_index("y"))


def pack_kernel(
    positions, queries, hist_keys, hist_values, new_keys, new_values, kv, kept, sent, tags, at, arrived
):
    core, line = own_place()
    first = pltpu.make_async_copy(positions, at, arrived.at[6])
    copies = [
        pltpu.make_async_copy(hist_keys, kv.at[0, pl.ds(0, HISTORY)], arrived.at[0]),
        pltpu.make_async_copy(hist_values, kv.at[1, pl.ds(0, HISTORY)], arrived.at[1]),
        pltpu.make_async_copy(new_keys, kv.at[0, pl.ds(HISTORY, NEWT)], arrived.at[2]),
        pltpu.make_async_copy(new_values, kv.at[1, pl.ds(HISTORY, NEWT)], arrived.at[3]),
        pltpu.make_async_copy(queries.at[:, :, core], kept, arrived.at[4]),
        pltpu.make_async_copy(queries.at[:, :, 1 - core], sent, arrived.at[5]),
    ]
    for copy in [first] + copies:
        copy.start()
    first.wait()
    lane = lax.broadcasted_iota(jnp.int32, (NEWT, HD), 1)
    row = lax.broadcasted_iota(jnp.int32, (8, HD), 0)
    key_tag = jnp.zeros((NEWT, HD), jnp.int32)
    for i in range(NEWT):
        key_tag = jnp.where(lane == line * NEWT + i, at[i], key_tag)
    for side, digit in enumerate((key_tag // 32, key_tag % 32)):
        kv[side, HISTORY + NEWT :, :] = digit.astype(jnp.float32).astype(jnp.bfloat16)
    query_tag = jnp.zeros((8, HD), jnp.int32)
    for i in range(TOKENS):
        position = at[lax.axis_index("x") * TOKENS + i]
        query_tag = jnp.where(row == i, position // 32, query_tag)
        query_tag = jnp.where(row == TOKENS + i, position % 32, query_tag)
    tags[...] = query_tag.astype(jnp.float32).astype(jnp.bfloat16)
    for copy in copies:
        copy.wait()


def spread_kernel(kept, received, tags, out, blocks, done):
    core = lax.axis_index("c")
    for x in range(XN):
        for owner, array in ((core, kept), (1 - core, received)):
            first = pl.multiple_of(owner * OWN * GROUP, OWN * GROUP)
            blocks[x, pl.ds(first, OWN * GROUP), :] = array[:, x].reshape(OWN * GROUP, HD)
        blocks[x, BLOCK:, :] = tags[...]
    copies = [
        pltpu.make_async_copy(blocks, out.at[pl.ds(line * XN, XN)], done.at[line]) for line in range(LINE)
    ]
    for copy in copies:
        copy.start()
    for copy in copies:
        copy.wait()


def join_kernel(own, lower, upper, three, two):
    for i, block in enumerate((own, lower, upper)):
        three[i] = block[...]
        if i < 2:
            two[i] = block[...]


def attend_kernel(page_slots, own, lower, upper, above, below, q, out, keys, values, scores):
    core, line = own_place()
    ctx = lax.axis_index("z") * YN + lax.axis_index("y")
    stride = jnp.where(core == 0, YN, 1)
    values[:, HD:] = jnp.ones((KEYS, HD), jnp.bfloat16)
    blocks = [own, lower, upper] + [above.at[i] for i in range(3)] + [below.at[i] for i in range(2)]
    high = jnp.zeros((NEWT, HD), jnp.float32)
    low = jnp.zeros((NEWT, HD), jnp.float32)
    count = jnp.int32(0)
    for block, offset in zip(blocks, OFFSETS, strict=True):
        source_line = lax.rem(line + offset + LINE, LINE)
        source = ctx + (source_line - line) * stride
        other = lax.rem(source + ZN * YN // 2, ZN * YN)
        first = pl.multiple_of(source_line * NEWT, NEWT)
        keys[pl.ds(first, NEWT), :] = block[0, HISTORY : HISTORY + NEWT, :]
        values[pl.ds(first, NEWT), :HD] = block[1, HISTORY : HISTORY + NEWT, :]
        high += block[0, HISTORY + NEWT :, :].astype(jnp.float32)
        low += block[1, HISTORY + NEWT :, :].astype(jnp.float32)
        candidates = [page_slots[2 * source], page_slots[2 * source + 1]]
        candidates += [page_slots[2 * other], page_slots[2 * other + 1]]
        for s in range(SLOTS):
            slot = source * SLOTS + s
            live = functools.reduce(jnp.logical_or, [candidate == slot for candidate in candidates])
            to = pl.multiple_of(FRESH + count * PAGE, PAGE)
            keys[pl.ds(to, PAGE), :] = block[0, s * PAGE : (s + 1) * PAGE, :]
            values[pl.ds(to, PAGE), :HD] = block[1, s * PAGE : (s + 1) * PAGE, :]
            count += live.astype(jnp.int32)
    key_at = (high * 32.0 + low)[0:1]
    places = functools.reduce(lambda size, less: jnp.where(count <= less, less, size), SIZES[-2::-1], SIZES[-1])

    def repeat(i, carry):
        here = pl.ds(pl.multiple_of(FRESH + i * PAGE, PAGE), PAGE)
        keys[here, :] = keys[FRESH : FRESH + PAGE, :]
        values[here, :] = jnp.zeros((PAGE, 2 * HD), jnp.bfloat16)
        return carry

    lax.fori_loop(count, places, repeat, 0)

    def chunks(pages):
        end = FRESH + pages * PAGE
        return [(start, min(CHUNK, end - start)) for start in range(0, end, CHUNK)]

    def score(part, side, pages):
        here = pl.ds(part * STEP_BLOCKS, STEP_BLOCKS)
        rows = q[here, :BLOCK, :].reshape(ROWS, HD)
        tags = q[here, BLOCK:, :].astype(jnp.float32)
        query_at = tags[:, :TOKENS, :] * 32.0 + tags[:, TOKENS:, :]
        hidden = jnp.where(key_at <= query_at, 0.0, LOWEST)
        bias = jnp.broadcast_to(hidden[:, :, None, :], (STEP_BLOCKS, TOKENS, GROUP, HD)).reshape(ROWS, HD)
        top = None
        for start, size in chunks(pages):
            product = lax.dot_general(
                rows, keys[start : start + size, :], (((1,), (1,)), ((), ())), preferred_element_type=jnp.float32
            )
            for j in range(0, size, HD):
                piece = product[:, j : j + HD]
                if start + j == 0:
                    piece = piece + bias
                scores[side, :, start + j : start + j + HD] = piece
                top = piece if top is None else jnp.maximum(top, piece)
        return top

    def weigh(part, side, pages, top):
        here = pl.ds(part * STEP_BLOCKS, STEP_BLOCKS)
        top = jnp.max(top, axis=1, keepdims=True) * TO_BITS
        summed = jnp.zeros((ROWS, 2 * HD), jnp.float32)
        for start, size in chunks(pages):
            weights = jnp.exp2(scores[side, :, start : start + size] * TO_BITS - top).astype(jnp.bfloat16)
            summed += jnp.dot(weights, values[start : start + size, :], preferred_element_type=jnp.float32)
        total = summed[:, HD:]
        out[here, :BLOCK, :] = (summed[:, :HD] / total).astype(jnp.bfloat16).reshape(STEP_BLOCKS, BLOCK, HD)
        level = (top + jnp.log2(total)).reshape(STEP_BLOCKS, BLOCK, HD)
        row = lax.broadcasted_iota(jnp.int32, (STEP_BLOCKS, BLOCK, HD), 1)
        lane = lax.broadcasted_iota(jnp.int32, (STEP_BLOCKS, BLOCK, HD), 2)
        level = jnp.sum(jnp.where(row == lane, level, 0.0), axis=1, keepdims=True)
        high = level.astype(jnp.bfloat16).astype(jnp.float32)
        rest = level - high
        middle = rest.astype(jnp.bfloat16).astype(jnp.float32)
        zeros = jnp.zeros((STEP_BLOCKS, 5, HD), jnp.float32)
        out[here, BLOCK:, :] = jnp.concatenate([high, middle, rest - middle, zeros], axis=1).astype(jnp.bfloat16)

    def attend_to(pages):
        def pair(i, carry):
            tops = [score(2 * i + side, side, pages) for side in range(2)]
            for side in range(2):
                weigh(2 * i + side, side, pages, tops[side])
            return carry

        lax.fori_loop(0, PARTS // 2, pair, 0)

    for pages in SIZES:
        pl.when(places == pages)(functools.partial(attend_to, pages))


def attend(page_slots, pieces, q):
    return call(
        attend_kernel,
        bf16(BLOCKS, WIRE, HD),
        megabytes=20,
        flops=2300000000,
        moved=5000000,
        in_specs=[SMEM] + [VMEM] * 6,
        scratch_shapes=[
            pltpu.VMEM((KEYS, HD), jnp.bfloat16),
            pltpu.VMEM((KEYS, 2 * HD), jnp.bfloat16),
            pltpu.VMEM((2, ROWS, KEYS), jnp.float32),
        ],
    )(page_slots, *pieces, q)


def combine_kernel(other, parts, out, merged_rows):
    owner = lax.axis_index("c") ^ other
    tags = parts[:, BLOCK:, :].astype(jnp.float32)
    level = tags[:, 0:1, :] + tags[:, 1:2, :] + tags[:, 2:3, :]
    level = level.reshape(LINE, XN, 1, HD)
    weight = jnp.exp2(level - jnp.max(level, axis=0, keepdims=True))
    weight = weight / jnp.sum(weight, axis=0, keepdims=True)
    row = lax.broadcasted_iota(jnp.int32, (BLOCK, HD), 0)
    lane = lax.broadcasted_iota(jnp.int32, (BLOCK, HD), 1)
    for x in range(XN):
        merged = jnp.zeros((BLOCK, HD), jnp.float32)
        for line in range(LINE):
            column = jnp.sum(jnp.where(row == lane, weight[line, x], 0.0), axis=1, keepdims=True)
            merged += column * parts[line * XN + x, :BLOCK, :].astype(jnp.float32)
        merged_rows[x] = merged.astype(jnp.bfloat16)
    for t in range(OWN):
        for x in range(XN):
            first = pl.multiple_of((owner * OWN + t) * GROUP, GROUP)
            out[t, x] = merged_rows[x, pl.ds(first, GROUP), :]


def finish_kernel(kept, received, out):
    core = lax.axis_index("c")
    for array, parity in ((kept, core), (received, 1 - core)):
        for t in range(OWN):
            for x in range(XN):
                first = pl.multiple_of((CN * x + parity) * GROUP, GROUP)
                out[t, pl.ds(first, GROUP), :] = array[t, x]


def body(queries, new_keys, new_values, new_positions, hist_keys, hist_values, page_slots):
    half = bf16(OWN, XN, GROUP, HD)
    sources = [
        new_positions,
        queries.reshape(OWN, XN, CN, GROUP, HD),
        hist_keys.reshape(HISTORY, HD),
        hist_values.reshape(HISTORY, HD),
        new_keys.reshape(NEWT, HD),
        new_values.reshape(NEWT, HD),
    ]
    kv, q_kept, q_sent, tags = call(
        pack_kernel,
        (bf16(2, KV_ROWS, HD), half, half, bf16(8, HD)),
        in_specs=[HBM] * 6,
        scratch_shapes=[pltpu.SMEM((NEWT,), jnp.int32), pltpu.SemaphoreType.DMA((7,))],
    )(*(pltpu.with_memory_space_constraint(source, pltpu.HBM) for source in sources))
    q_received = lax.ppermute(q_sent, ALL, SWAP)
    kv, q_received = lax.optimization_barrier((kv, q_received))
    lower = lax.ppermute(kv, ALL, along(3))
    upper = lax.ppermute(kv, ALL, along(-2))
    q = call(
        spread_kernel,
        bf16(BLOCKS, WIRE, HD),
        out_specs=HBM,
        scratch_shapes=[pltpu.VMEM((XN, WIRE, HD), jnp.bfloat16), pltpu.SemaphoreType.DMA((LINE,))],
    )(q_kept, q_received, tags)
    q = lax.all_to_all(q, ALL, split_axis=0, concat_axis=0, axis_index_groups=CROSS, tiled=True)
    three, two = call(join_kernel, (bf16(3, 2, KV_ROWS, HD), bf16(2, 2, KV_ROWS, HD)), flops=JOIN)(kv, lower, upper)
    above = lax.ppermute(three, ALL, along(-1))
    below = lax.ppermute(two, ALL, along(1))
    parts = attend(page_slots, (kv, lower, upper, above, below), q)
    parts = lax.all_to_all(parts, ALL, split_axis=0, concat_axis=0, axis_index_groups=CROSS, tiled=True)

    def combined(other):
        return call(
            functools.partial(combine_kernel, other),
            half,
            scratch_shapes=[pltpu.VMEM((XN, BLOCK, HD), jnp.bfloat16)],
        )(parts)

    received = lax.ppermute(combined(1), ALL, SWAP)
    return call(finish_kernel, bf16(OWN, HEADS, HD))(combined(0), received)


def solution(mesh):
    split = Mesh(mesh.devices.reshape(ZN, YN, XN, CN), ALL)
    ctx, kvh = ("z", "y"), ("x", "c")
    in_specs = (
        P(ctx + kvh, None, None),
        P(ctx, kvh, None),
        P(ctx, kvh, None),
        P(ctx),
        P(ctx, None, kvh, None),
        P(ctx, None, kvh, None),
        P(),
    )
    return jax.shard_map(body, mesh=split, in_specs=in_specs, out_specs=P(ctx + kvh, None, None), check_vma=False)
```

```python
import functools
import math

import jax
import jax.numpy as jnp
import numpy as np
from jax import lax
from jax.experimental import pallas as pl
from jax.experimental.pallas import tpu as pltpu
from jax.sharding import Mesh, PartitionSpec as P

ZN, YN, XN, CN = 8, 8, 4, 2
LINE = 8
ALL = ("z", "y", "x", "c")
HEADS, GROUP, HD, PAGE, SLOTS, NEWT = 128, 16, 128, 128, 3, 16
HISTORY = SLOTS * PAGE
KV_ROWS = HISTORY + 2 * NEWT
FRESH = LINE * NEWT
MOST_PAGES = LINE * SLOTS
KEYS = FRESH + MOST_PAGES * PAGE
OWN = 2
TOKENS = OWN * CN
BLOCK = TOKENS * GROUP
WIRE = BLOCK + 8
BLOCKS = LINE * XN
STEP_BLOCKS = 8
ROWS = STEP_BLOCKS * BLOCK
PARTS = BLOCKS // STEP_BLOCKS
CHUNK = 512
SIZES = (16, 18, 20, 24)
OFFSETS = (0, -3, 2, 1, -2, 3, -1, -4)
TO_BITS = math.log2(math.e) / math.sqrt(HD)
LOWEST = -1e30
JOIN = 30000000000

IDS = np.arange(ZN * YN * XN * CN).reshape(ZN, YN, XN, CN)
CROSS = [IDS[z, :, :, 0].ravel().tolist() for z in range(ZN)] + [IDS[:, y, :, 1].ravel().tolist() for y in range(YN)]


def along(distance):
    route = []
    for z in range(ZN):
        for y in range(YN):
            for x in range(XN):
                route.append((int(IDS[z, y, x, 0]), int(IDS[(z + distance) % ZN, y, x, 0])))
                route.append((int(IDS[z, y, x, 1]), int(IDS[z, (y + distance) % YN, x, 1])))
    return route


SWAP = [(int(i), int(i) ^ 1) for i in IDS.ravel()]


def call(kernel, out_shape, megabytes=16, flops=1000000, moved=800000, **options):
    return pl.pallas_call(
        kernel,
        out_shape=out_shape,
        compiler_params=pltpu.CompilerParams(vmem_limit_bytes=megabytes * 1024 * 1024),
        cost_estimate=pl.CostEstimate(flops=flops, bytes_accessed=moved, transcendentals=flops // 500),
        **options,
    )


def bf16(*shape):
    return jax.ShapeDtypeStruct(shape, jnp.bfloat16)


SMEM = pl.BlockSpec(memory_space=pltpu.SMEM)
HBM = pl.BlockSpec(memory_space=pltpu.HBM)
VMEM = pl.BlockSpec(memory_space=pltpu.VMEM)


def own_place():
    core = lax.axis_index("c")
    return core, jnp.where(core == 0, lax.axis_index("z"), lax.axis_index("y"))


def pack_kernel(
    positions, queries, hist_keys, hist_values, new_keys, new_values, kv, kept, sent, tags, at, arrived
):
    core, line = own_place()
    first = pltpu.make_async_copy(positions, at, arrived.at[6])
    copies = [
        pltpu.make_async_copy(hist_keys, kv.at[0, pl.ds(0, HISTORY)], arrived.at[0]),
        pltpu.make_async_copy(hist_values, kv.at[1, pl.ds(0, HISTORY)], arrived.at[1]),
        pltpu.make_async_copy(new_keys, kv.at[0, pl.ds(HISTORY, NEWT)], arrived.at[2]),
        pltpu.make_async_copy(new_values, kv.at[1, pl.ds(HISTORY, NEWT)], arrived.at[3]),
        pltpu.make_async_copy(queries.at[:, :, core], kept, arrived.at[4]),
        pltpu.make_async_copy(queries.at[:, :, 1 - core], sent, arrived.at[5]),
    ]
    for copy in [first] + copies:
        copy.start()
    first.wait()
    lane = lax.broadcasted_iota(jnp.int32, (NEWT, HD), 1)
    row = lax.broadcasted_iota(jnp.int32, (8, HD), 0)
    key_tag = jnp.zeros((NEWT, HD), jnp.int32)
    for i in range(NEWT):
        key_tag = jnp.where(lane == line * NEWT + i, at[i], key_tag)
    for side, digit in enumerate((key_tag // 32, key_tag % 32)):
        kv[side, HISTORY + NEWT :, :] = digit.astype(jnp.float32).astype(jnp.bfloat16)
    query_tag = jnp.zeros((8, HD), jnp.int32)
    for i in range(TOKENS):
        position = at[lax.axis_index("x") * TOKENS + i]
        query_tag = jnp.where(row == i, position // 32, query_tag)
        query_tag = jnp.where(row == TOKENS + i, position % 32, query_tag)
    tags[...] = query_tag.astype(jnp.float32).astype(jnp.bfloat16)
    for copy in copies:
        copy.wait()


def spread_kernel(kept, received, tags, out, blocks, done):
    core = lax.axis_index("c")
    for x in range(XN):
        for owner, array in ((core, kept), (1 - core, received)):
            first = pl.multiple_of(owner * OWN * GROUP, OWN * GROUP)
            blocks[x, pl.ds(first, OWN * GROUP), :] = array[:, x].reshape(OWN * GROUP, HD)
        blocks[x, BLOCK:, :] = tags[...]
    copies = [
        pltpu.make_async_copy(blocks, out.at[pl.ds(line * XN, XN)], done.at[line]) for line in range(LINE)
    ]
    for copy in copies:
        copy.start()
    for copy in copies:
        copy.wait()


def join_kernel(own, lower, upper, down, up):
    for i, half in enumerate((own.at[0], lower.at[0], lower.at[1], upper.at[0], upper.at[1])):
        down[i] = half[...]
    for i, half in enumerate((own.at[0], own.at[1], lower.at[0], lower.at[1], upper.at[1])):
        up[i] = half[...]


def attend_kernel(page_slots, own, lower, upper, above, below, q, out, keys, values, scores):
    core, line = own_place()
    ctx = lax.axis_index("z") * YN + lax.axis_index("y")
    stride = jnp.where(core == 0, YN, 1)
    values[:, HD:] = jnp.ones((KEYS, HD), jnp.bfloat16)
    blocks = [(block.at[0], block.at[1]) for block in (own, lower, upper)]
    blocks += [(above.at[0], below.at[4]), (above.at[1], above.at[2]), (above.at[3], above.at[4])]
    blocks += [(below.at[0], below.at[1]), (below.at[2], below.at[3])]
    high = jnp.zeros((NEWT, HD), jnp.float32)
    low = jnp.zeros((NEWT, HD), jnp.float32)
    count = jnp.int32(0)
    for (block_keys, block_values), offset in zip(blocks, OFFSETS, strict=True):
        source_line = lax.rem(line + offset + LINE, LINE)
        source = ctx + (source_line - line) * stride
        other = lax.rem(source + ZN * YN // 2, ZN * YN)
        first = pl.multiple_of(source_line * NEWT, NEWT)
        keys[pl.ds(first, NEWT), :] = block_keys[HISTORY : HISTORY + NEWT, :]
        values[pl.ds(first, NEWT), :HD] = block_values[HISTORY : HISTORY + NEWT, :]
        high += block_keys[HISTORY + NEWT :, :].astype(jnp.float32)
        low += block_values[HISTORY + NEWT :, :].astype(jnp.float32)
        candidates = [page_slots[2 * source], page_slots[2 * source + 1]]
        candidates += [page_slots[2 * other], page_slots[2 * other + 1]]
        for s in range(SLOTS):
            slot = source * SLOTS + s
            live = functools.reduce(jnp.logical_or, [candidate == slot for candidate in candidates])
            to = pl.multiple_of(FRESH + count * PAGE, PAGE)
            keys[pl.ds(to, PAGE), :] = block_keys[s * PAGE : (s + 1) * PAGE, :]
            values[pl.ds(to, PAGE), :HD] = block_values[s * PAGE : (s + 1) * PAGE, :]
            count += live.astype(jnp.int32)
    key_at = (high * 32.0 + low)[0:1]
    places = functools.reduce(lambda size, less: jnp.where(count <= less, less, size), SIZES[-2::-1], SIZES[-1])

    def repeat(i, carry):
        here = pl.ds(pl.multiple_of(FRESH + i * PAGE, PAGE), PAGE)
        keys[here, :] = keys[FRESH : FRESH + PAGE, :]
        values[here, :] = jnp.zeros((PAGE, 2 * HD), jnp.bfloat16)
        return carry

    lax.fori_loop(count, places, repeat, 0)

    def chunks(pages):
        end = FRESH + pages * PAGE
        return [(start, min(CHUNK, end - start)) for start in range(0, end, CHUNK)]

    def score(part, side, pages):
        here = pl.ds(part * STEP_BLOCKS, STEP_BLOCKS)
        rows = q[here, :BLOCK, :].reshape(ROWS, HD)
        tags = q[here, BLOCK:, :].astype(jnp.float32)
        query_at = tags[:, :TOKENS, :] * 32.0 + tags[:, TOKENS:, :]
        hidden = jnp.where(key_at <= query_at, 0.0, LOWEST)
        bias = jnp.broadcast_to(hidden[:, :, None, :], (STEP_BLOCKS, TOKENS, GROUP, HD)).reshape(ROWS, HD)
        top = None
        for start, size in chunks(pages):
            product = lax.dot_general(
                rows, keys[start : start + size, :], (((1,), (1,)), ((), ())), preferred_element_type=jnp.float32
            )
            for j in range(0, size, HD):
                piece = product[:, j : j + HD]
                if start + j == 0:
                    piece = piece + bias
                scores[side, :, start + j : start + j + HD] = piece
                top = piece if top is None else jnp.maximum(top, piece)
        return top

    def weigh(part, side, pages, top):
        here = pl.ds(part * STEP_BLOCKS, STEP_BLOCKS)
        top = jnp.max(top, axis=1, keepdims=True) * TO_BITS
        summed = jnp.zeros((ROWS, 2 * HD), jnp.float32)
        for start, size in chunks(pages):
            weights = jnp.exp2(scores[side, :, start : start + size] * TO_BITS - top).astype(jnp.bfloat16)
            summed += jnp.dot(weights, values[start : start + size, :], preferred_element_type=jnp.float32)
        total = summed[:, HD:]
        out[here, :BLOCK, :] = (summed[:, :HD] / total).astype(jnp.bfloat16).reshape(STEP_BLOCKS, BLOCK, HD)
        level = (top + jnp.log2(total)).reshape(STEP_BLOCKS, BLOCK, HD)
        row = lax.broadcasted_iota(jnp.int32, (STEP_BLOCKS, BLOCK, HD), 1)
        lane = lax.broadcasted_iota(jnp.int32, (STEP_BLOCKS, BLOCK, HD), 2)
        level = jnp.sum(jnp.where(row == lane, level, 0.0), axis=1, keepdims=True)
        high = level.astype(jnp.bfloat16).astype(jnp.float32)
        rest = level - high
        middle = rest.astype(jnp.bfloat16).astype(jnp.float32)
        zeros = jnp.zeros((STEP_BLOCKS, 5, HD), jnp.float32)
        out[here, BLOCK:, :] = jnp.concatenate([high, middle, rest - middle, zeros], axis=1).astype(jnp.bfloat16)

    def attend_to(pages):
        def pair(i, carry):
            tops = [score(2 * i + side, side, pages) for side in range(2)]
            for side in range(2):
                weigh(2 * i + side, side, pages, tops[side])
            return carry

        lax.fori_loop(0, PARTS // 2, pair, 0)

    for pages in SIZES:
        pl.when(places == pages)(functools.partial(attend_to, pages))


def attend(page_slots, pieces, q):
    return call(
        attend_kernel,
        bf16(BLOCKS, WIRE, HD),
        megabytes=20,
        flops=2300000000,
        moved=5000000,
        in_specs=[SMEM] + [VMEM] * 6,
        scratch_shapes=[
            pltpu.VMEM((KEYS, HD), jnp.bfloat16),
            pltpu.VMEM((KEYS, 2 * HD), jnp.bfloat16),
            pltpu.VMEM((2, ROWS, KEYS), jnp.float32),
        ],
    )(page_slots, *pieces, q)


def combine_kernel(other, parts, out, merged_rows):
    owner = lax.axis_index("c") ^ other
    tags = parts[:, BLOCK:, :].astype(jnp.float32)
    level = tags[:, 0:1, :] + tags[:, 1:2, :] + tags[:, 2:3, :]
    level = level.reshape(LINE, XN, 1, HD)
    weight = jnp.exp2(level - jnp.max(level, axis=0, keepdims=True))
    weight = weight / jnp.sum(weight, axis=0, keepdims=True)
    row = lax.broadcasted_iota(jnp.int32, (BLOCK, HD), 0)
    lane = lax.broadcasted_iota(jnp.int32, (BLOCK, HD), 1)
    for x in range(XN):
        merged = jnp.zeros((BLOCK, HD), jnp.float32)
        for line in range(LINE):
            column = jnp.sum(jnp.where(row == lane, weight[line, x], 0.0), axis=1, keepdims=True)
            merged += column * parts[line * XN + x, :BLOCK, :].astype(jnp.float32)
        merged_rows[x] = merged.astype(jnp.bfloat16)
    for t in range(OWN):
        for x in range(XN):
            first = pl.multiple_of((owner * OWN + t) * GROUP, GROUP)
            out[t, x] = merged_rows[x, pl.ds(first, GROUP), :]


def finish_kernel(kept, received, out):
    core = lax.axis_index("c")
    for array, parity in ((kept, core), (received, 1 - core)):
        for t in range(OWN):
            for x in range(XN):
                first = pl.multiple_of((CN * x + parity) * GROUP, GROUP)
                out[t, pl.ds(first, GROUP), :] = array[t, x]


def body(queries, new_keys, new_values, new_positions, hist_keys, hist_values, page_slots):
    half = bf16(OWN, XN, GROUP, HD)
    sources = [
        new_positions,
        queries.reshape(OWN, XN, CN, GROUP, HD),
        hist_keys.reshape(HISTORY, HD),
        hist_values.reshape(HISTORY, HD),
        new_keys.reshape(NEWT, HD),
        new_values.reshape(NEWT, HD),
    ]
    kv, q_kept, q_sent, tags = call(
        pack_kernel,
        (bf16(2, KV_ROWS, HD), half, half, bf16(8, HD)),
        in_specs=[HBM] * 6,
        scratch_shapes=[pltpu.SMEM((NEWT,), jnp.int32), pltpu.SemaphoreType.DMA((7,))],
    )(*(pltpu.with_memory_space_constraint(source, pltpu.HBM) for source in sources))
    q_received = lax.ppermute(q_sent, ALL, SWAP)
    kv, q_received = lax.optimization_barrier((kv, q_received))
    lower = lax.ppermute(kv, ALL, along(3))
    upper = lax.ppermute(kv, ALL, along(-2))
    q = call(
        spread_kernel,
        bf16(BLOCKS, WIRE, HD),
        out_specs=HBM,
        scratch_shapes=[pltpu.VMEM((XN, WIRE, HD), jnp.bfloat16), pltpu.SemaphoreType.DMA((LINE,))],
    )(q_kept, q_received, tags)
    q = lax.all_to_all(q, ALL, split_axis=0, concat_axis=0, axis_index_groups=CROSS, tiled=True)
    halves = bf16(5, KV_ROWS, HD)
    down, up = call(join_kernel, (halves, halves), flops=JOIN)(kv, lower, upper)
    above = lax.ppermute(down, ALL, along(-1))
    below = lax.ppermute(up, ALL, along(1))
    parts = attend(page_slots, (kv, lower, upper, above, below), q)
    parts = lax.all_to_all(parts, ALL, split_axis=0, concat_axis=0, axis_index_groups=CROSS, tiled=True)

    def combined(other):
        return call(
            functools.partial(combine_kernel, other),
            half,
            scratch_shapes=[pltpu.VMEM((XN, BLOCK, HD), jnp.bfloat16)],
        )(parts)

    received = lax.ppermute(combined(1), ALL, SWAP)
    return call(finish_kernel, bf16(OWN, HEADS, HD))(combined(0), received)


def solution(mesh):
    split = Mesh(mesh.devices.reshape(ZN, YN, XN, CN), ALL)
    ctx, kvh = ("z", "y"), ("x", "c")
    in_specs = (
        P(ctx + kvh, None, None),
        P(ctx, kvh, None),
        P(ctx, kvh, None),
        P(ctx),
        P(ctx, None, kvh, None),
        P(ctx, None, kvh, None),
        P(),
    )
    return jax.shard_map(body, mesh=split, in_specs=in_specs, out_specs=P(ctx + kvh, None, None), check_vma=False)
```

```python
import functools
import math

import jax
import jax.numpy as jnp
import numpy as np
from jax import lax
from jax.experimental import pallas as pl
from jax.experimental.pallas import tpu as pltpu
from jax.sharding import Mesh, PartitionSpec as P

ZN, YN, XN, CN = 8, 8, 4, 2
LINE = 8
ALL = ("z", "y", "x", "c")
HEADS, GROUP, HD, PAGE, SLOTS, NEWT = 128, 16, 128, 128, 3, 16
HISTORY = SLOTS * PAGE
KV_ROWS = HISTORY + 2 * NEWT
FRESH = LINE * NEWT
MOST_PAGES = LINE * SLOTS
KEYS = FRESH + MOST_PAGES * PAGE
OWN = 2
TOKENS = OWN * CN
BLOCK = TOKENS * GROUP
WIRE = BLOCK + 8
BLOCKS = LINE * XN
STEP_BLOCKS = 8
ROWS = STEP_BLOCKS * BLOCK
PARTS = BLOCKS // STEP_BLOCKS
CHUNK = 512
SIZES = (16, 18, 20, 24)
OFFSETS = (0, -3, 2, 1, -2, 3, -1, -4)
TO_BITS = math.log2(math.e) / math.sqrt(HD)
LOWEST = -1e30
JOIN = 30000000000
SPREAD = 10000000000

IDS = np.arange(ZN * YN * XN * CN).reshape(ZN, YN, XN, CN)
CROSS = [IDS[z, :, :, 0].ravel().tolist() for z in range(ZN)] + [IDS[:, y, :, 1].ravel().tolist() for y in range(YN)]


def along(distance):
    route = []
    for z in range(ZN):
        for y in range(YN):
            for x in range(XN):
                route.append((int(IDS[z, y, x, 0]), int(IDS[(z + distance) % ZN, y, x, 0])))
                route.append((int(IDS[z, y, x, 1]), int(IDS[z, (y + distance) % YN, x, 1])))
    return route


SWAP = [(int(i), int(i) ^ 1) for i in IDS.ravel()]


def call(kernel, out_shape, megabytes=16, flops=1000000, moved=800000, **options):
    return pl.pallas_call(
        kernel,
        out_shape=out_shape,
        compiler_params=pltpu.CompilerParams(vmem_limit_bytes=megabytes * 1024 * 1024),
        cost_estimate=pl.CostEstimate(flops=flops, bytes_accessed=moved, transcendentals=flops // 500),
        **options,
    )


def bf16(*shape):
    return jax.ShapeDtypeStruct(shape, jnp.bfloat16)


SMEM = pl.BlockSpec(memory_space=pltpu.SMEM)
HBM = pl.BlockSpec(memory_space=pltpu.HBM)
VMEM = pl.BlockSpec(memory_space=pltpu.VMEM)


def own_place():
    core = lax.axis_index("c")
    return core, jnp.where(core == 0, lax.axis_index("z"), lax.axis_index("y"))


def pack_kernel(
    positions, queries, hist_keys, hist_values, new_keys, new_values, kv, kept, sent, tags, at, arrived
):
    core, line = own_place()
    first = pltpu.make_async_copy(positions, at, arrived.at[6])
    copies = [
        pltpu.make_async_copy(hist_keys, kv.at[0, pl.ds(0, HISTORY)], arrived.at[0]),
        pltpu.make_async_copy(hist_values, kv.at[1, pl.ds(0, HISTORY)], arrived.at[1]),
        pltpu.make_async_copy(new_keys, kv.at[0, pl.ds(HISTORY, NEWT)], arrived.at[2]),
        pltpu.make_async_copy(new_values, kv.at[1, pl.ds(HISTORY, NEWT)], arrived.at[3]),
        pltpu.make_async_copy(queries.at[:, :, core], kept, arrived.at[4]),
        pltpu.make_async_copy(queries.at[:, :, 1 - core], sent, arrived.at[5]),
    ]
    for copy in [first] + copies:
        copy.start()
    first.wait()
    lane = lax.broadcasted_iota(jnp.int32, (NEWT, HD), 1)
    row = lax.broadcasted_iota(jnp.int32, (8, HD), 0)
    key_tag = jnp.zeros((NEWT, HD), jnp.int32)
    for i in range(NEWT):
        key_tag = jnp.where(lane == line * NEWT + i, at[i], key_tag)
    for side, digit in enumerate((key_tag // 32, key_tag % 32)):
        kv[side, HISTORY + NEWT :, :] = digit.astype(jnp.float32).astype(jnp.bfloat16)
    query_tag = jnp.zeros((8, HD), jnp.int32)
    for i in range(TOKENS):
        position = at[lax.axis_index("x") * TOKENS + i]
        query_tag = jnp.where(row == i, position // 32, query_tag)
        query_tag = jnp.where(row == TOKENS + i, position % 32, query_tag)
    tags[...] = query_tag.astype(jnp.float32).astype(jnp.bfloat16)
    for copy in copies:
        copy.wait()


def spread_kernel(kept, received, tags, out, blocks, done):
    core = lax.axis_index("c")
    for x in range(XN):
        for owner, array in ((core, kept), (1 - core, received)):
            first = pl.multiple_of(owner * OWN * GROUP, OWN * GROUP)
            blocks[x, pl.ds(first, OWN * GROUP), :] = array[:, x].reshape(OWN * GROUP, HD)
        blocks[x, BLOCK:, :] = tags[...]
    copies = [
        pltpu.make_async_copy(blocks, out.at[pl.ds(line * XN, XN)], done.at[line]) for line in range(LINE)
    ]
    for copy in copies:
        copy.start()
    for copy in copies:
        copy.wait()


def join_kernel(own, lower, upper, three, two):
    for i, block in enumerate((own, lower, upper)):
        three[i] = block[...]
        if i < 2:
            two[i] = block[...]


def attend_kernel(page_slots, own, lower, upper, above, below, q, out, keys, values, scores):
    core, line = own_place()
    ctx = lax.axis_index("z") * YN + lax.axis_index("y")
    stride = jnp.where(core == 0, YN, 1)
    values[:, HD:] = jnp.ones((KEYS, HD), jnp.bfloat16)
    blocks = [own, lower, upper] + [above.at[i] for i in range(3)] + [below.at[i] for i in range(2)]
    high = jnp.zeros((NEWT, HD), jnp.float32)
    low = jnp.zeros((NEWT, HD), jnp.float32)
    count = jnp.int32(0)
    for block, offset in zip(blocks, OFFSETS, strict=True):
        source_line = lax.rem(line + offset + LINE, LINE)
        source = ctx + (source_line - line) * stride
        other = lax.rem(source + ZN * YN // 2, ZN * YN)
        first = pl.multiple_of(source_line * NEWT, NEWT)
        keys[pl.ds(first, NEWT), :] = block[0, HISTORY : HISTORY + NEWT, :]
        values[pl.ds(first, NEWT), :HD] = block[1, HISTORY : HISTORY + NEWT, :]
        high += block[0, HISTORY + NEWT :, :].astype(jnp.float32)
        low += block[1, HISTORY + NEWT :, :].astype(jnp.float32)
        candidates = [page_slots[2 * source], page_slots[2 * source + 1]]
        candidates += [page_slots[2 * other], page_slots[2 * other + 1]]
        for s in range(SLOTS):
            slot = source * SLOTS + s
            live = functools.reduce(jnp.logical_or, [candidate == slot for candidate in candidates])
            to = pl.multiple_of(FRESH + count * PAGE, PAGE)
            keys[pl.ds(to, PAGE), :] = block[0, s * PAGE : (s + 1) * PAGE, :]
            values[pl.ds(to, PAGE), :HD] = block[1, s * PAGE : (s + 1) * PAGE, :]
            count += live.astype(jnp.int32)
    key_at = (high * 32.0 + low)[0:1]
    places = functools.reduce(lambda size, less: jnp.where(count <= less, less, size), SIZES[-2::-1], SIZES[-1])

    def repeat(i, carry):
        here = pl.ds(pl.multiple_of(FRESH + i * PAGE, PAGE), PAGE)
        keys[here, :] = keys[FRESH : FRESH + PAGE, :]
        values[here, :] = jnp.zeros((PAGE, 2 * HD), jnp.bfloat16)
        return carry

    lax.fori_loop(count, places, repeat, 0)

    def chunks(pages):
        end = FRESH + pages * PAGE
        return [(start, min(CHUNK, end - start)) for start in range(0, end, CHUNK)]

    def score(part, side, pages):
        here = pl.ds(part * STEP_BLOCKS, STEP_BLOCKS)
        rows = q[here, :BLOCK, :].reshape(ROWS, HD)
        tags = q[here, BLOCK:, :].astype(jnp.float32)
        query_at = tags[:, :TOKENS, :] * 32.0 + tags[:, TOKENS:, :]
        hidden = jnp.where(key_at <= query_at, 0.0, LOWEST)
        bias = jnp.broadcast_to(hidden[:, :, None, :], (STEP_BLOCKS, TOKENS, GROUP, HD)).reshape(ROWS, HD)
        top = None
        for start, size in chunks(pages):
            product = lax.dot_general(
                rows, keys[start : start + size, :], (((1,), (1,)), ((), ())), preferred_element_type=jnp.float32
            )
            for j in range(0, size, HD):
                piece = product[:, j : j + HD]
                if start + j == 0:
                    piece = piece + bias
                scores[side, :, start + j : start + j + HD] = piece
                top = piece if top is None else jnp.maximum(top, piece)
        return top

    def weigh(part, side, pages, top):
        here = pl.ds(part * STEP_BLOCKS, STEP_BLOCKS)
        top = jnp.max(top, axis=1, keepdims=True) * TO_BITS
        summed = jnp.zeros((ROWS, 2 * HD), jnp.float32)
        for start, size in chunks(pages):
            weights = jnp.exp2(scores[side, :, start : start + size] * TO_BITS - top).astype(jnp.bfloat16)
            summed += jnp.dot(weights, values[start : start + size, :], preferred_element_type=jnp.float32)
        total = summed[:, HD:]
        out[here, :BLOCK, :] = (summed[:, :HD] / total).astype(jnp.bfloat16).reshape(STEP_BLOCKS, BLOCK, HD)
        level = (top + jnp.log2(total)).reshape(STEP_BLOCKS, BLOCK, HD)
        row = lax.broadcasted_iota(jnp.int32, (STEP_BLOCKS, BLOCK, HD), 1)
        lane = lax.broadcasted_iota(jnp.int32, (STEP_BLOCKS, BLOCK, HD), 2)
        level = jnp.sum(jnp.where(row == lane, level, 0.0), axis=1, keepdims=True)
        high = level.astype(jnp.bfloat16).astype(jnp.float32)
        rest = level - high
        middle = rest.astype(jnp.bfloat16).astype(jnp.float32)
        zeros = jnp.zeros((STEP_BLOCKS, 5, HD), jnp.float32)
        out[here, BLOCK:, :] = jnp.concatenate([high, middle, rest - middle, zeros], axis=1).astype(jnp.bfloat16)

    def attend_to(pages):
        def pair(i, carry):
            tops = [score(2 * i + side, side, pages) for side in range(2)]
            for side in range(2):
                weigh(2 * i + side, side, pages, tops[side])
            return carry

        lax.fori_loop(0, PARTS // 2, pair, 0)

    for pages in SIZES:
        pl.when(places == pages)(functools.partial(attend_to, pages))


def attend(page_slots, pieces, q):
    return call(
        attend_kernel,
        bf16(BLOCKS, WIRE, HD),
        megabytes=20,
        flops=2300000000,
        moved=5000000,
        in_specs=[SMEM] + [VMEM] * 6,
        scratch_shapes=[
            pltpu.VMEM((KEYS, HD), jnp.bfloat16),
            pltpu.VMEM((KEYS, 2 * HD), jnp.bfloat16),
            pltpu.VMEM((2, ROWS, KEYS), jnp.float32),
        ],
    )(page_slots, *pieces, q)


def combine_kernel(other, parts, out, merged_rows):
    owner = lax.axis_index("c") ^ other
    tags = parts[:, BLOCK:, :].astype(jnp.float32)
    level = tags[:, 0:1, :] + tags[:, 1:2, :] + tags[:, 2:3, :]
    level = level.reshape(LINE, XN, 1, HD)
    weight = jnp.exp2(level - jnp.max(level, axis=0, keepdims=True))
    weight = weight / jnp.sum(weight, axis=0, keepdims=True)
    row = lax.broadcasted_iota(jnp.int32, (BLOCK, HD), 0)
    lane = lax.broadcasted_iota(jnp.int32, (BLOCK, HD), 1)
    for x in range(XN):
        merged = jnp.zeros((BLOCK, HD), jnp.float32)
        for line in range(LINE):
            column = jnp.sum(jnp.where(row == lane, weight[line, x], 0.0), axis=1, keepdims=True)
            merged += column * parts[line * XN + x, :BLOCK, :].astype(jnp.float32)
        merged_rows[x] = merged.astype(jnp.bfloat16)
    for t in range(OWN):
        for x in range(XN):
            first = pl.multiple_of((owner * OWN + t) * GROUP, GROUP)
            out[t, x] = merged_rows[x, pl.ds(first, GROUP), :]


def finish_kernel(kept, received, out):
    core = lax.axis_index("c")
    for array, parity in ((kept, core), (received, 1 - core)):
        for t in range(OWN):
            for x in range(XN):
                first = pl.multiple_of((CN * x + parity) * GROUP, GROUP)
                out[t, pl.ds(first, GROUP), :] = array[t, x]


def body(queries, new_keys, new_values, new_positions, hist_keys, hist_values, page_slots):
    half = bf16(OWN, XN, GROUP, HD)
    sources = [
        new_positions,
        queries.reshape(OWN, XN, CN, GROUP, HD),
        hist_keys.reshape(HISTORY, HD),
        hist_values.reshape(HISTORY, HD),
        new_keys.reshape(NEWT, HD),
        new_values.reshape(NEWT, HD),
    ]
    kv, q_kept, q_sent, tags = call(
        pack_kernel,
        (bf16(2, KV_ROWS, HD), half, half, bf16(8, HD)),
        in_specs=[HBM] * 6,
        scratch_shapes=[pltpu.SMEM((NEWT,), jnp.int32), pltpu.SemaphoreType.DMA((7,))],
    )(*(pltpu.with_memory_space_constraint(source, pltpu.HBM) for source in sources))
    q_received = lax.ppermute(q_sent, ALL, SWAP)
    lower = lax.ppermute(kv, ALL, along(3))
    upper = lax.ppermute(kv, ALL, along(-2))
    q = call(
        spread_kernel,
        bf16(BLOCKS, WIRE, HD),
        flops=SPREAD,
        out_specs=HBM,
        scratch_shapes=[pltpu.VMEM((XN, WIRE, HD), jnp.bfloat16), pltpu.SemaphoreType.DMA((LINE,))],
    )(q_kept, q_received, tags)
    q = lax.all_to_all(q, ALL, split_axis=0, concat_axis=0, axis_index_groups=CROSS, tiled=True)
    three, two = call(join_kernel, (bf16(3, 2, KV_ROWS, HD), bf16(2, 2, KV_ROWS, HD)), flops=JOIN)(kv, lower, upper)
    above = lax.ppermute(three, ALL, along(-1))
    below = lax.ppermute(two, ALL, along(1))
    parts = attend(page_slots, (kv, lower, upper, above, below), q)
    parts = lax.all_to_all(parts, ALL, split_axis=0, concat_axis=0, axis_index_groups=CROSS, tiled=True)

    def combined(other):
        return call(
            functools.partial(combine_kernel, other),
            half,
            scratch_shapes=[pltpu.VMEM((XN, BLOCK, HD), jnp.bfloat16)],
        )(parts)

    received = lax.ppermute(combined(1), ALL, SWAP)
    return call(finish_kernel, bf16(OWN, HEADS, HD))(combined(0), received)


def solution(mesh):
    split = Mesh(mesh.devices.reshape(ZN, YN, XN, CN), ALL)
    ctx, kvh = ("z", "y"), ("x", "c")
    in_specs = (
        P(ctx + kvh, None, None),
        P(ctx, kvh, None),
        P(ctx, kvh, None),
        P(ctx),
        P(ctx, None, kvh, None),
        P(ctx, None, kvh, None),
        P(),
    )
    return jax.shard_map(body, mesh=split, in_specs=in_specs, out_specs=P(ctx + kvh, None, None), check_vma=False)
```

```python
import functools
import math

import jax
import jax.numpy as jnp
import numpy as np
from jax import lax
from jax.experimental import pallas as pl
from jax.experimental.pallas import tpu as pltpu
from jax.sharding import Mesh, PartitionSpec as P

ZN, YN, XN, CN = 8, 8, 4, 2
LINE = 8
ALL = ("z", "y", "x", "c")
HEADS, GROUP, HD, PAGE, SLOTS, NEWT = 128, 16, 128, 128, 3, 16
HISTORY = SLOTS * PAGE
KV_ROWS = HISTORY + 2 * NEWT
FRESH = LINE * NEWT
MOST_PAGES = LINE * SLOTS
KEYS = FRESH + MOST_PAGES * PAGE
OWN = 2
TOKENS = OWN * CN
BLOCK = TOKENS * GROUP
WIRE = BLOCK + 8
BLOCKS = LINE * XN
STEP_BLOCKS = 8
ROWS = STEP_BLOCKS * BLOCK
PARTS = BLOCKS // STEP_BLOCKS
CHUNK = 512
SIZES = (16, 18, 20, 24)
OFFSETS = (0, 3, -2, 1, 4, -1, 2, -3)
TO_BITS = math.log2(math.e) / math.sqrt(HD)
LOWEST = -1e30
JOIN = 30000000000
SPREAD = 10000000000

IDS = np.arange(ZN * YN * XN * CN).reshape(ZN, YN, XN, CN)
CROSS = [IDS[z, :, :, 0].ravel().tolist() for z in range(ZN)] + [IDS[:, y, :, 1].ravel().tolist() for y in range(YN)]


def along(distance):
    route = []
    for z in range(ZN):
        for y in range(YN):
            for x in range(XN):
                route.append((int(IDS[z, y, x, 0]), int(IDS[(z + distance) % ZN, y, x, 0])))
                route.append((int(IDS[z, y, x, 1]), int(IDS[z, (y + distance) % YN, x, 1])))
    return route


SWAP = [(int(i), int(i) ^ 1) for i in IDS.ravel()]


def call(kernel, out_shape, megabytes=16, flops=1000000, moved=800000, **options):
    return pl.pallas_call(
        kernel,
        out_shape=out_shape,
        compiler_params=pltpu.CompilerParams(vmem_limit_bytes=megabytes * 1024 * 1024),
        cost_estimate=pl.CostEstimate(flops=flops, bytes_accessed=moved, transcendentals=flops // 500),
        **options,
    )


def bf16(*shape):
    return jax.ShapeDtypeStruct(shape, jnp.bfloat16)


SMEM = pl.BlockSpec(memory_space=pltpu.SMEM)
HBM = pl.BlockSpec(memory_space=pltpu.HBM)
VMEM = pl.BlockSpec(memory_space=pltpu.VMEM)


def own_place():
    core = lax.axis_index("c")
    return core, jnp.where(core == 0, lax.axis_index("z"), lax.axis_index("y"))


def pack_kernel(
    positions, queries, hist_keys, hist_values, new_keys, new_values, kv, kept, sent, tags, at, arrived
):
    core, line = own_place()
    first = pltpu.make_async_copy(positions, at, arrived.at[6])
    copies = [
        pltpu.make_async_copy(hist_keys, kv.at[0, pl.ds(0, HISTORY)], arrived.at[0]),
        pltpu.make_async_copy(hist_values, kv.at[1, pl.ds(0, HISTORY)], arrived.at[1]),
        pltpu.make_async_copy(new_keys, kv.at[0, pl.ds(HISTORY, NEWT)], arrived.at[2]),
        pltpu.make_async_copy(new_values, kv.at[1, pl.ds(HISTORY, NEWT)], arrived.at[3]),
        pltpu.make_async_copy(queries.at[:, :, core], kept, arrived.at[4]),
        pltpu.make_async_copy(queries.at[:, :, 1 - core], sent, arrived.at[5]),
    ]
    for copy in [first] + copies:
        copy.start()
    first.wait()
    lane = lax.broadcasted_iota(jnp.int32, (NEWT, HD), 1)
    row = lax.broadcasted_iota(jnp.int32, (8, HD), 0)
    key_tag = jnp.zeros((NEWT, HD), jnp.int32)
    for i in range(NEWT):
        key_tag = jnp.where(lane == line * NEWT + i, at[i], key_tag)
    for side, digit in enumerate((key_tag // 32, key_tag % 32)):
        kv[side, HISTORY + NEWT :, :] = digit.astype(jnp.float32).astype(jnp.bfloat16)
    query_tag = jnp.zeros((8, HD), jnp.int32)
    for i in range(TOKENS):
        position = at[lax.axis_index("x") * TOKENS + i]
        query_tag = jnp.where(row == i, position // 32, query_tag)
        query_tag = jnp.where(row == TOKENS + i, position % 32, query_tag)
    tags[...] = query_tag.astype(jnp.float32).astype(jnp.bfloat16)
    for copy in copies:
        copy.wait()


def spread_kernel(kept, received, tags, out, blocks, done):
    core = lax.axis_index("c")
    for x in range(XN):
        for owner, array in ((core, kept), (1 - core, received)):
            first = pl.multiple_of(owner * OWN * GROUP, OWN * GROUP)
            blocks[x, pl.ds(first, OWN * GROUP), :] = array[:, x].reshape(OWN * GROUP, HD)
        blocks[x, BLOCK:, :] = tags[...]
    copies = [
        pltpu.make_async_copy(blocks, out.at[pl.ds(line * XN, XN)], done.at[line]) for line in range(LINE)
    ]
    for copy in copies:
        copy.start()
    for copy in copies:
        copy.wait()


def join_kernel(own, lower, upper, three, two):
    for i, block in enumerate((own, lower, upper)):
        three[i] = block[...]
        if i > 0:
            two[i - 1] = block[...]


def attend_kernel(page_slots, own, lower, upper, above, below, q, out, keys, values, scores):
    core, line = own_place()
    ctx = lax.axis_index("z") * YN + lax.axis_index("y")
    stride = jnp.where(core == 0, YN, 1)
    values[:, HD:] = jnp.ones((KEYS, HD), jnp.bfloat16)
    blocks = [own, lower, upper] + [above.at[i] for i in range(3)] + [below.at[i] for i in range(2)]
    high = jnp.zeros((NEWT, HD), jnp.float32)
    low = jnp.zeros((NEWT, HD), jnp.float32)
    count = jnp.int32(0)
    for block, offset in zip(blocks, OFFSETS, strict=True):
        source_line = lax.rem(line + offset + LINE, LINE)
        source = ctx + (source_line - line) * stride
        other = lax.rem(source + ZN * YN // 2, ZN * YN)
        first = pl.multiple_of(source_line * NEWT, NEWT)
        keys[pl.ds(first, NEWT), :] = block[0, HISTORY : HISTORY + NEWT, :]
        values[pl.ds(first, NEWT), :HD] = block[1, HISTORY : HISTORY + NEWT, :]
        high += block[0, HISTORY + NEWT :, :].astype(jnp.float32)
        low += block[1, HISTORY + NEWT :, :].astype(jnp.float32)
        candidates = [page_slots[2 * source], page_slots[2 * source + 1]]
        candidates += [page_slots[2 * other], page_slots[2 * other + 1]]
        for s in range(SLOTS):
            slot = source * SLOTS + s
            live = functools.reduce(jnp.logical_or, [candidate == slot for candidate in candidates])
            to = pl.multiple_of(FRESH + count * PAGE, PAGE)
            keys[pl.ds(to, PAGE), :] = block[0, s * PAGE : (s + 1) * PAGE, :]
            values[pl.ds(to, PAGE), :HD] = block[1, s * PAGE : (s + 1) * PAGE, :]
            count += live.astype(jnp.int32)
    key_at = (high * 32.0 + low)[0:1]
    places = functools.reduce(lambda size, less: jnp.where(count <= less, less, size), SIZES[-2::-1], SIZES[-1])

    def repeat(i, carry):
        here = pl.ds(pl.multiple_of(FRESH + i * PAGE, PAGE), PAGE)
        keys[here, :] = keys[FRESH : FRESH + PAGE, :]
        values[here, :] = jnp.zeros((PAGE, 2 * HD), jnp.bfloat16)
        return carry

    lax.fori_loop(count, places, repeat, 0)

    def chunks(pages):
        end = FRESH + pages * PAGE
        return [(start, min(CHUNK, end - start)) for start in range(0, end, CHUNK)]

    def score(part, side, pages):
        here = pl.ds(part * STEP_BLOCKS, STEP_BLOCKS)
        rows = q[here, :BLOCK, :].reshape(ROWS, HD)
        tags = q[here, BLOCK:, :].astype(jnp.float32)
        query_at = tags[:, :TOKENS, :] * 32.0 + tags[:, TOKENS:, :]
        hidden = jnp.where(key_at <= query_at, 0.0, LOWEST)
        bias = jnp.broadcast_to(hidden[:, :, None, :], (STEP_BLOCKS, TOKENS, GROUP, HD)).reshape(ROWS, HD)
        top = None
        for start, size in chunks(pages):
            product = lax.dot_general(
                rows, keys[start : start + size, :], (((1,), (1,)), ((), ())), preferred_element_type=jnp.float32
            )
            for j in range(0, size, HD):
                piece = product[:, j : j + HD]
                if start + j == 0:
                    piece = piece + bias
                scores[side, :, start + j : start + j + HD] = piece
                top = piece if top is None else jnp.maximum(top, piece)
        return top

    def weigh(part, side, pages, top):
        here = pl.ds(part * STEP_BLOCKS, STEP_BLOCKS)
        top = jnp.max(top, axis=1, keepdims=True) * TO_BITS
        summed = jnp.zeros((ROWS, 2 * HD), jnp.float32)
        for start, size in chunks(pages):
            weights = jnp.exp2(scores[side, :, start : start + size] * TO_BITS - top).astype(jnp.bfloat16)
            summed += jnp.dot(weights, values[start : start + size, :], preferred_element_type=jnp.float32)
        total = summed[:, HD:]
        out[here, :BLOCK, :] = (summed[:, :HD] / total).astype(jnp.bfloat16).reshape(STEP_BLOCKS, BLOCK, HD)
        level = (top + jnp.log2(total)).reshape(STEP_BLOCKS, BLOCK, HD)
        row = lax.broadcasted_iota(jnp.int32, (STEP_BLOCKS, BLOCK, HD), 1)
        lane = lax.broadcasted_iota(jnp.int32, (STEP_BLOCKS, BLOCK, HD), 2)
        level = jnp.sum(jnp.where(row == lane, level, 0.0), axis=1, keepdims=True)
        high = level.astype(jnp.bfloat16).astype(jnp.float32)
        rest = level - high
        middle = rest.astype(jnp.bfloat16).astype(jnp.float32)
        zeros = jnp.zeros((STEP_BLOCKS, 5, HD), jnp.float32)
        out[here, BLOCK:, :] = jnp.concatenate([high, middle, rest - middle, zeros], axis=1).astype(jnp.bfloat16)

    def attend_to(pages):
        def pair(i, carry):
            tops = [score(2 * i + side, side, pages) for side in range(2)]
            for side in range(2):
                weigh(2 * i + side, side, pages, tops[side])
            return carry

        lax.fori_loop(0, PARTS // 2, pair, 0)

    for pages in SIZES:
        pl.when(places == pages)(functools.partial(attend_to, pages))


def attend(page_slots, pieces, q):
    return call(
        attend_kernel,
        bf16(BLOCKS, WIRE, HD),
        megabytes=20,
        flops=2300000000,
        moved=5000000,
        in_specs=[SMEM] + [VMEM] * 6,
        scratch_shapes=[
            pltpu.VMEM((KEYS, HD), jnp.bfloat16),
            pltpu.VMEM((KEYS, 2 * HD), jnp.bfloat16),
            pltpu.VMEM((2, ROWS, KEYS), jnp.float32),
        ],
    )(page_slots, *pieces, q)


def combine_kernel(other, parts, out, merged_rows):
    owner = lax.axis_index("c") ^ other
    tags = parts[:, BLOCK:, :].astype(jnp.float32)
    level = tags[:, 0:1, :] + tags[:, 1:2, :] + tags[:, 2:3, :]
    level = level.reshape(LINE, XN, 1, HD)
    weight = jnp.exp2(level - jnp.max(level, axis=0, keepdims=True))
    weight = weight / jnp.sum(weight, axis=0, keepdims=True)
    row = lax.broadcasted_iota(jnp.int32, (BLOCK, HD), 0)
    lane = lax.broadcasted_iota(jnp.int32, (BLOCK, HD), 1)
    for x in range(XN):
        merged = jnp.zeros((BLOCK, HD), jnp.float32)
        for line in range(LINE):
            column = jnp.sum(jnp.where(row == lane, weight[line, x], 0.0), axis=1, keepdims=True)
            merged += column * parts[line * XN + x, :BLOCK, :].astype(jnp.float32)
        merged_rows[x] = merged.astype(jnp.bfloat16)
    for t in range(OWN):
        for x in range(XN):
            first = pl.multiple_of((owner * OWN + t) * GROUP, GROUP)
            out[t, x] = merged_rows[x, pl.ds(first, GROUP), :]


def finish_kernel(kept, received, out):
    core = lax.axis_index("c")
    for array, parity in ((kept, core), (received, 1 - core)):
        for t in range(OWN):
            for x in range(XN):
                first = pl.multiple_of((CN * x + parity) * GROUP, GROUP)
                out[t, pl.ds(first, GROUP), :] = array[t, x]


def body(queries, new_keys, new_values, new_positions, hist_keys, hist_values, page_slots):
    half = bf16(OWN, XN, GROUP, HD)
    sources = [
        new_positions,
        queries.reshape(OWN, XN, CN, GROUP, HD),
        hist_keys.reshape(HISTORY, HD),
        hist_values.reshape(HISTORY, HD),
        new_keys.reshape(NEWT, HD),
        new_values.reshape(NEWT, HD),
    ]
    kv, q_kept, q_sent, tags = call(
        pack_kernel,
        (bf16(2, KV_ROWS, HD), half, half, bf16(8, HD)),
        in_specs=[HBM] * 6,
        scratch_shapes=[pltpu.SMEM((NEWT,), jnp.int32), pltpu.SemaphoreType.DMA((7,))],
    )(*(pltpu.with_memory_space_constraint(source, pltpu.HBM) for source in sources))
    q_received = lax.ppermute(q_sent, ALL, SWAP)
    lower = lax.ppermute(kv, ALL, along(-3))
    upper = lax.ppermute(kv, ALL, along(2))
    q = call(
        spread_kernel,
        bf16(BLOCKS, WIRE, HD),
        flops=SPREAD,
        out_specs=HBM,
        scratch_shapes=[pltpu.VMEM((XN, WIRE, HD), jnp.bfloat16), pltpu.SemaphoreType.DMA((LINE,))],
    )(q_kept, q_received, tags)
    q = lax.all_to_all(q, ALL, split_axis=0, concat_axis=0, axis_index_groups=CROSS, tiled=True)
    three, two = call(join_kernel, (bf16(3, 2, KV_ROWS, HD), bf16(2, 2, KV_ROWS, HD)), flops=JOIN)(kv, lower, upper)
    above = lax.ppermute(three, ALL, along(-1))
    below = lax.ppermute(two, ALL, along(1))
    parts = attend(page_slots, (kv, lower, upper, above, below), q)
    parts = lax.all_to_all(parts, ALL, split_axis=0, concat_axis=0, axis_index_groups=CROSS, tiled=True)

    def combined(other):
        return call(
            functools.partial(combine_kernel, other),
            half,
            scratch_shapes=[pltpu.VMEM((XN, BLOCK, HD), jnp.bfloat16)],
        )(parts)

    received = lax.ppermute(combined(1), ALL, SWAP)
    return call(finish_kernel, bf16(OWN, HEADS, HD))(combined(0), received)


def solution(mesh):
    split = Mesh(mesh.devices.reshape(ZN, YN, XN, CN), ALL)
    ctx, kvh = ("z", "y"), ("x", "c")
    in_specs = (
        P(ctx + kvh, None, None),
        P(ctx, kvh, None),
        P(ctx, kvh, None),
        P(ctx),
        P(ctx, None, kvh, None),
        P(ctx, None, kvh, None),
        P(),
    )
    return jax.shard_map(body, mesh=split, in_specs=in_specs, out_specs=P(ctx + kvh, None, None), check_vma=False)
```
